512 devices in a mesh: dp: 32 (over y, x), fsdp: 16 (over z, core).
Axes of the slice: x: 4, y: 8, z: 8, core: 2. Of those that a mesh axis runs over, the one named last changes fastest.
Arguments:
- grad: bfloat16 [32, 2048, 4096], P('dp', 'fsdp'), may hold values from -8 to 8
- error: bfloat16 [32, 2048, 4096], P('dp', 'fsdp'), may hold values from -3 to 3
- q_warm: float32 [64, 4096], P(None, 'fsdp'), may hold values from -5 to 5
Outputs:
- error_next: bfloat16 [32, 2048, 4096], P('dp', 'fsdp')
- decompressed: bfloat16 [2048, 4096], P('fsdp', 'dp')
- q_next: float32 [64, 4096], P(None, 'fsdp')
The draws below stay inside these ranges and needn't reach their ends.
All inputs are finite; a program needn't handle non-finite values.
Results may differ from the reference program's by a relative error of at most 0.0074.
Values may be sent and summed in bfloat16 or wider, within the bound.
No kernel may reach another device: no remote copies, remote signals or barrier semaphores. Data moves between devices by JAX's collectives and lax.ppermute only.
A program may use at most 64 MiB of HBM per device.

```python
import math
import jax
import jax.numpy as jnp
from jax import lax

C = 4096
RANK = 64
ROWS = 2048
REPLICAS = 32
N_DP = 32


def draw_grad(key, part):
    key = jax.random.fold_in(key, 11)
    k_rows, k_cols, k_shared, k_noise = jax.random.split(key, 4)
    row_scale = jnp.exp(jax.random.uniform(k_rows, (ROWS,), jnp.float32, math.log(0.5), math.log(2.0)))
    col_scale = jnp.exp(jax.random.uniform(k_cols, (C,), jnp.float32, math.log(0.5), math.log(2.0)))
    shared = jnp.clip(jax.random.normal(k_shared, (ROWS, C), jnp.float32), -5.0, 5.0)
    noise = 0.7 * jnp.clip(jax.random.normal(k_noise, (REPLICAS, ROWS, C), jnp.float32), -5.0, 5.0)
    value = row_scale[None, :, None] * col_scale[None, None, :] * (shared[None] + noise)
    return jnp.clip(value, -8.0, 8.0).astype(jnp.bfloat16)


def level_of(key, extent, pieces, least, high):
    def one(dim, shards_of):
        steps = jax.random.uniform(jax.random.fold_in(jax.random.fold_in(key, 6), dim), (shards_of,), jnp.float32, least / len(pieces), high / len(pieces))
        return jnp.repeat(jnp.exp(steps), extent[dim] // shards_of).reshape((-1,) + (1,) * (len(extent) - dim - 1))

    gain = one(*pieces[0])
    for cut in pieces[1:]:
        gain = gain * one(*cut)
    return gain


def gaussian(own_key, extent, spread, most, cuts=(), dtype=jnp.bfloat16):
    result = jax.random.normal(own_key, extent, jnp.float32) * spread
    if len(cuts) > 0:
        result = level_of(own_key, extent, cuts, -0.22, 0.18) * result
    return jnp.clip(result, min=-most, max=most).astype(dtype)


def setup_inputs(seed: int = 0) -> dict:
    streams_of = jax.random.split(jax.random.key(seed), 4)
    return {
        "grad": draw_grad(jax.random.fold_in(streams_of[3], 71), 0),
        "error": gaussian(streams_of[1], (REPLICAS, ROWS, C), 0.5, 3.0, ((0, 32), (1, 16))),
        "q_warm": gaussian(streams_of[2], (RANK, C), 1.0, 5.0, ((1, 16),), jnp.float32),
    }


def merge_pair(grad_one, error_one):
    merged = (grad_one.astype(jnp.float32) + error_one.astype(jnp.float32)).astype(jnp.bfloat16)
    return lax.optimization_barrier(merged)

def reference(grad, error, q_warm):
    warm_bf = q_warm.astype(jnp.bfloat16)

    def p_step(running, inputs):
        merged = merge_pair(inputs[0], inputs[1])
        return (running + jnp.dot(merged.astype(jnp.float32), warm_bf.T.astype(jnp.float32), preferred_element_type=jnp.float32), None)
    p_total, _ = lax.scan(p_step, jnp.zeros((ROWS, RANK), jnp.float32), (grad, error))
    p_mean = p_total / N_DP
    gram_matrix = jnp.dot(p_mean.T, p_mean, precision=lax.Precision.HIGHEST)
    chol_lower = jnp.linalg.cholesky(gram_matrix)
    p_ortho = lax.linalg.triangular_solve(chol_lower, p_mean, left_side=False, lower=True, transpose_a=True)
    ortho_bf = p_ortho.astype(jnp.bfloat16)

    def q_step(running, inputs):
        merged = merge_pair(inputs[0], inputs[1])
        return (running + jnp.dot(ortho_bf.T.astype(jnp.float32), merged.astype(jnp.float32), preferred_element_type=jnp.float32), None)
    q_total, _ = lax.scan(q_step, jnp.zeros((RANK, C), jnp.float32), (grad, error))
    q_next = q_total / N_DP
    approx = jnp.dot(ortho_bf.astype(jnp.float32), q_next.astype(jnp.bfloat16).astype(jnp.float32), preferred_element_type=jnp.float32)

    def new_error(inputs):
        merged = merge_pair(inputs[0], inputs[1])
        return (merged.astype(jnp.float32) - approx).astype(jnp.bfloat16)
    error_next = lax.map(new_error, (grad, error))
    return (error_next, approx.astype(jnp.bfloat16), q_next)
```

```python
import jax
import jax.numpy as jnp
from jax import lax
from jax.sharding import Mesh, PartitionSpec as P

Y, X, Z, CORES = 8, 4, 8, 2
DP = ("y", "x")
FSDP = ("z", "core")
EXACT = lax.Precision.HIGHEST


def copies_to_all(value, axis, count):
    return lax.all_to_all(jnp.broadcast_to(value[None], (count,) + value.shape), axis, 0, 0)


def on_device(grad, error, q_warm):
    rows, col_count = grad.shape[1:]
    rank = q_warm.shape[0]
    dp_count = Y * X
    cols = col_count // dp_count
    merged = (grad[0].astype(jnp.float32) + error[0].astype(jnp.float32)).astype(jnp.bfloat16)
    merged = lax.optimization_barrier(merged)

    by_column = merged.reshape(rows, dp_count, cols).transpose(1, 0, 2)
    landed = lax.all_to_all(by_column, DP, 0, 0)

    warm = lax.all_gather(q_warm.astype(jnp.bfloat16), FSDP, axis=1, tiled=True)
    left = lax.dot_general(
        warm, merged, (((1,), (1,)), ((), ())), preferred_element_type=jnp.float32
    )
    left = copies_to_all(left, "x", X).sum(0)
    left = copies_to_all(left, "y", Y).sum(0) / dp_count

    mean_cols = landed.astype(jnp.float32).sum(0) / dp_count
    q_terms = jnp.dot(left, mean_cols, precision=EXACT)
    gram = lax.dot_general(left, left, (((1,), (1,)), ((), ())), precision=EXACT)
    both = jnp.concatenate([q_terms, gram], axis=1)
    both = lax.psum(both, "core")
    both = copies_to_all(both, "z", Z).sum(0)
    q_sum, gram = both[:, :cols], both[:, cols:]

    chol_lower = jnp.linalg.cholesky(gram)
    inverse = lax.linalg.triangular_solve(
        chol_lower, jnp.eye(rank, dtype=jnp.float32), left_side=True, lower=True
    )
    q_mine = jnp.dot(inverse, q_sum, precision=EXACT).astype(jnp.bfloat16)
    q_all = copies_to_all(q_mine, DP, dp_count)
    ortho = jnp.dot(inverse, left, precision=EXACT).astype(jnp.bfloat16)
    q_bf = q_all.transpose(1, 0, 2).reshape(rank, col_count)

    def rebuild(right):
        return lax.dot_general(
            ortho, right, (((0,), (0,)), ((), ())), preferred_element_type=jnp.float32
        )

    decompressed = rebuild(q_mine).astype(jnp.bfloat16)
    error_next = (merged.astype(jnp.float32) - rebuild(q_bf)).astype(jnp.bfloat16)[None]
    shard = col_count // (Z * CORES)
    q_next = lax.dynamic_slice_in_dim(q_bf, lax.axis_index(FSDP) * shard, shard, 1)
    return (error_next, decompressed, q_next.astype(jnp.float32))


def solution(mesh):
    grid = Mesh(mesh.devices.reshape(Y, X, Z, CORES), DP + FSDP)
    return jax.shard_map(
        on_device,
        mesh=grid,
        in_specs=(P(DP, FSDP, None), P(DP, FSDP, None), P(None, FSDP)),
        out_specs=(P(DP, FSDP, None), P(FSDP, DP), P(None, FSDP)),
        check_vma=False,
    )
```

```python
import jax
import jax.numpy as jnp
from jax import lax
from jax.experimental import pallas as pl
from jax.experimental.pallas import tpu as pltpu
from jax.sharding import Mesh, PartitionSpec as P

Y, X, Z, CORES = 8, 4, 8, 2
DP = ("y", "x")
FSDP = ("z", "core")
EXACT = lax.Precision.HIGHEST
F32, BF16 = jnp.float32, jnp.bfloat16
VMEM = pl.BlockSpec(memory_space=pltpu.VMEM)
SMEM = pl.BlockSpec(memory_space=pltpu.SMEM)
PARAMS = pltpu.CompilerParams(vmem_limit_bytes=32 * 1024 * 1024)
RANK = 64


def call(kernel, out, *operands, scalars=0):
    specs = [SMEM] * scalars + [VMEM] * (len(operands) - scalars)
    many = isinstance(out, (list, tuple))
    return pl.pallas_call(
        kernel,
        out_shape=out,
        in_specs=specs,
        out_specs=[VMEM] * len(out) if many else VMEM,
        compiler_params=PARAMS,
    )(*operands)


def shape(dtype, *dims):
    return jax.ShapeDtypeStruct(dims, dtype)


def left_kernel(landed_ref, warm_ref, out_ref):
    _, rows, col_count = landed_ref.shape
    wide = col_count // Y
    stacked = landed_ref[...].reshape(X * rows, col_count)
    every = lax.dot_general(
        stacked, warm_ref[...], (((1,), (1,)), ((), ())), preferred_element_type=F32
    )
    left = every[:rows]
    for x in range(1, X):
        left = left + every[x * rows : (x + 1) * rows]
    high = left.astype(BF16)
    rest = left - high.astype(F32)
    middle = rest.astype(BF16)
    low = (rest - middle.astype(F32)).astype(BF16)
    first = jnp.concatenate([high, middle], axis=1)
    second = jnp.concatenate([low, jnp.zeros_like(low)], axis=1)
    for y in range(Y):
        span = pl.ds(y * wide, wide)
        total = landed_ref[0, :, span].astype(F32)
        for x in range(1, X):
            total = total + landed_ref[x, :, span].astype(F32)
        out_ref[y, :, :wide] = total.astype(BF16)
        out_ref[y, :, wide : wide + 2 * RANK] = first
        out_ref[y, :, wide + 2 * RANK :] = second


def terms_kernel(landed_ref, out_ref):
    total = landed_ref[0].astype(F32)
    for y in range(1, Y):
        total = total + landed_ref[y].astype(F32)
    wide = total.shape[1] - 4 * RANK
    total = total * (1.0 / (X * Y))
    mean = total[:, :wide]
    left = (
        total[:, wide : wide + RANK]
        + total[:, wide + RANK : wide + 2 * RANK]
        + total[:, wide + 2 * RANK : wide + 3 * RANK]
    )
    over_rows = (((0,), (0,)), ((), ()))
    q_terms = lax.dot_general(left, mean, over_rows, precision=EXACT, preferred_element_type=F32)
    gram = lax.dot_general(left, left, over_rows, precision=EXACT, preferred_element_type=F32)
    cols = wide // X
    half, quarter = RANK // 2, RANK // 4
    rows = left.shape[0] // 2
    folded_left = jnp.concatenate([left[:rows], left[rows:]], axis=1)
    for core in range(CORES):
        own = gram[core * half : (core + 1) * half]
        folded = jnp.concatenate([own[:quarter], own[quarter:]], axis=1)
        for x in range(X):
            peer = x * CORES + core
            out_ref[peer, :half] = q_terms[core * half : (core + 1) * half, x * cols : (x + 1) * cols]
            out_ref[peer, half : half + quarter] = folded
            out_ref[peer, half + quarter :] = folded_left


def factor_kernel(where_ref, sums_ref, left_ref, q_ref, ortho_ref):
    half, quarter = RANK // 2, RANK // 4
    lane = lax.broadcasted_iota(jnp.int32, (8, 2 * RANK), 1)
    sub = lax.broadcasted_iota(jnp.int32, (8, 2 * RANK), 0)
    blocks = []
    for b in range(RANK // 8):
        core, at = divmod(b, 4)
        raw = sums_ref[core, half + 8 * (at % 2) : half + 8 * (at % 2) + 8, :]
        if at >= 2:
            raw = pltpu.roll(raw, RANK, 1)
        unit = (lane == sub + RANK + 8 * b).astype(F32)
        blocks.append(jnp.where(lane < RANK, raw, unit))

    def lane_copy(value, column):
        return jnp.broadcast_to(value[:, column : column + 1], value.shape)

    def row_copy(value, row):
        return jnp.broadcast_to(value[row : row + 1], value.shape)

    inverse_rows = []
    for b in range(RANK // 8):
        here = blocks[b]
        columns = [lane_copy(here, 8 * b + j) for j in range(8)]
        later = [
            [lane_copy(blocks[t], 8 * b + j) for j in range(8)] for t in range(b + 1, RANK // 8)
        ]
        scales = jnp.zeros_like(here)
        for j in range(8):
            pivot = row_copy(columns[j], j)
            recip = 1.0 / pivot
            scales = jnp.where(sub == j, recip, scales)
            factor = jnp.where(sub > j, columns[j] * recip, 0.0)
            here = here - factor * row_copy(here, j)
            for other in range(j + 1, 8):
                columns[other] = columns[other] - factor * row_copy(columns[other], j)
        inverse_rows.append(here * jnp.sqrt(scales))
        if b + 1 == RANK // 8:
            break
        solved = here * scales
        uppers = [columns[j] * scales for j in range(8)]
        for j in range(7, 0, -1):
            factor = jnp.where(sub < j, uppers[j], 0.0)
            solved = solved - factor * row_copy(solved, j)
        for t in range(b + 1, RANK // 8):
            update = later[t - b - 1][0] * row_copy(solved, 0)
            for j in range(1, 8):
                update = update + later[t - b - 1][j] * row_copy(solved, j)
            blocks[t] = blocks[t] - update
    inverse = jnp.concatenate(inverse_rows, axis=0)[:, RANK:]

    q_sum = jnp.concatenate([sums_ref[0, :half], sums_ref[1, :half]], axis=0)
    q_mine = jnp.dot(inverse, q_sum, precision=EXACT, preferred_element_type=F32).astype(BF16)
    for peer in range(q_ref.shape[0]):
        q_ref[peer] = q_mine
    core = where_ref[2]
    pieces = []
    for x in range(X):
        piece = left_ref[x * CORES + core, half + quarter :]
        pieces += [piece[:, :RANK], piece[:, RANK:]]
    left = jnp.concatenate(pieces, axis=0)
    ortho_ref[...] = lax.dot_general(
        left, inverse, (((1,), (1,)), ((), ())), precision=EXACT, preferred_element_type=F32
    ).astype(BF16)


def rebuild_kernel(where_ref, q_ref, ortho_ref, merged_ref, error_ref, own_ref, q_next_ref):
    ortho = ortho_ref[...]
    count, _, cols = q_ref.shape
    for d in range(count):
        span = pl.ds(d * cols, cols)
        approx = jnp.dot(ortho, q_ref[d], preferred_element_type=F32)
        error_ref[0, :, span] = (merged_ref[:, span].astype(F32) - approx).astype(BF16)
    own_ref[...] = jnp.dot(ortho, q_ref[where_ref[0]], preferred_element_type=F32).astype(BF16)
    each = q_next_ref.shape[1] // cols
    for i in range(each):
        q_next_ref[:, i * cols : (i + 1) * cols] = q_ref[where_ref[1] * each + i].astype(F32)


def on_device(grad, error, q_warm):
    rows, col_count = grad.shape[1:]
    dp_count = Y * X
    cols = col_count // dp_count
    wide = col_count // Y
    part = rows // X
    merged = (grad[0].astype(F32) + error[0].astype(F32)).astype(BF16)
    merged = lax.optimization_barrier(merged)

    landed = lax.all_to_all(merged.reshape(X, part, col_count), "x", 0, 0)
    warm = lax.all_gather(q_warm.astype(BF16), FSDP, axis=1, tiled=True)
    to_y = call(left_kernel, shape(BF16, Y, part, wide + 4 * RANK), landed, warm)
    to_pair = call(
        terms_kernel, shape(F32, X * CORES, RANK, cols), lax.all_to_all(to_y, "y", 0, 0)
    )
    landed = lax.all_to_all(to_pair, ("x", "core"), 0, 0)
    kept = RANK // 2 + RANK // 4
    sums = landed[:, :kept].sum(0)
    sums = lax.all_to_all(jnp.broadcast_to(sums[None], (Z,) + sums.shape), "z", 0, 0).sum(0)
    sums = lax.all_gather(sums, "core")

    where = jnp.stack([lax.axis_index(DP), lax.axis_index(FSDP), lax.axis_index("core")])
    q_copies, ortho = call(
        factor_kernel,
        (shape(BF16, dp_count, RANK, cols), shape(BF16, rows, RANK)),
        where, sums, landed, scalars=1,
    )
    q_all = lax.all_to_all(q_copies, DP, 0, 0)
    return call(
        rebuild_kernel,
        (
            shape(BF16, 1, rows, col_count),
            shape(BF16, rows, cols),
            shape(F32, RANK, q_warm.shape[1]),
        ),
        where, q_all, ortho, merged, scalars=1,
    )


def solution(mesh):
    grid = Mesh(mesh.devices.reshape(Y, X, Z, CORES), DP + FSDP)
    return jax.shard_map(
        on_device,
        mesh=grid,
        in_specs=(P(DP, FSDP, None), P(DP, FSDP, None), P(None, FSDP)),
        out_specs=(P(DP, FSDP, None), P(FSDP, DP), P(None, FSDP)),
        check_vma=False,
    )
```

```python
import jax
import jax.numpy as jnp
from jax import lax
from jax.experimental import pallas as pl
from jax.experimental.pallas import tpu as pltpu
from jax.sharding import Mesh, PartitionSpec as P

YH, YL, X, Z, CORES = 4, 2, 4, 8, 2
NEAR = ("yl", "x")
DP = ("yh", "yl", "x")
FSDP = ("z", "core")
NEARS = YL * X
CUTS = 8
SPANS = 4
REPLICAS = YH * YL * X
RANK = 64
HALF, QUARTER = RANK // 2, RANK // 4
EXACT = lax.Precision.HIGHEST
F32, BF16 = jnp.float32, jnp.bfloat16
VMEM = pl.BlockSpec(memory_space=pltpu.VMEM)
ANY = pl.BlockSpec(memory_space=pl.ANY)
LIMIT = 32 * 1024 * 1024


def call(kernel, out, *operands):
    many = isinstance(out, (list, tuple))
    return pl.pallas_call(
        kernel,
        out_shape=out,
        in_specs=[VMEM] * len(operands),
        out_specs=[VMEM] * len(out) if many else VMEM,
        compiler_params=pltpu.CompilerParams(vmem_limit_bytes=LIMIT),
    )(*operands)


def shape(dtype, *dims):
    return jax.ShapeDtypeStruct(dims, dtype)


def merge_kernel(grad_hbm, error_hbm, merged_hbm, grad, error, merged, in_sems, out_sems):
    part = merged.shape[0] // CUTS
    copies = []
    for i in range(CUTS):
        span = pl.ds(i * part, part)
        copies.append(
            (
                pltpu.make_async_copy(grad_hbm.at[0, span], grad.at[span], in_sems.at[0, i]),
                pltpu.make_async_copy(error_hbm.at[0, span], error.at[span], in_sems.at[1, i]),
                pltpu.make_async_copy(merged.at[span], merged_hbm.at[span], out_sems.at[i]),
            )
        )
        copies[i][0].start()
        copies[i][1].start()
    for i in range(CUTS):
        copies[i][0].wait()
        copies[i][1].wait()
        span = pl.ds(i * part, part)
        merged[span] = (grad[span].astype(F32) + error[span].astype(F32)).astype(BF16)
        copies[i][2].start()
    for i in range(CUTS):
        copies[i][2].wait()


def merge(grad, error):
    _, rows, col_count = grad.shape
    return pl.pallas_call(
        merge_kernel,
        out_shape=shape(BF16, rows, col_count),
        in_specs=[ANY, ANY],
        out_specs=ANY,
        scratch_shapes=[pltpu.VMEM((rows, col_count), BF16)] * 3
        + [pltpu.SemaphoreType.DMA((2, CUTS)), pltpu.SemaphoreType.DMA((CUTS,))],
        compiler_params=pltpu.CompilerParams(vmem_limit_bytes=60 * 1024 * 1024),
    )(grad, error)


def left_kernel(landed_ref, warm_ref, out_ref):
    _, rows, col_count = landed_ref.shape
    wide = col_count // YH
    stacked = landed_ref[...].reshape(NEARS * rows, col_count)
    every = lax.dot_general(
        stacked, warm_ref[...], (((1,), (1,)), ((), ())), preferred_element_type=F32
    )
    left = every[:rows]
    for peer in range(1, NEARS):
        left = left + every[peer * rows : (peer + 1) * rows]
    high = left.astype(BF16)
    rest = left - high.astype(F32)
    middle = rest.astype(BF16)
    low = (rest - middle.astype(F32)).astype(BF16)
    first = jnp.concatenate([high, middle], axis=1)
    second = jnp.concatenate([low, jnp.zeros_like(low)], axis=1)
    for y in range(YH):
        span = pl.ds(y * wide, wide)
        total = landed_ref[0, :, span].astype(F32)
        for peer in range(1, NEARS):
            total = total + landed_ref[peer, :, span].astype(F32)
        out_ref[y, :, :wide] = total.astype(BF16)
        out_ref[y, :, wide : wide + 2 * RANK] = first
        out_ref[y, :, wide + 2 * RANK :] = second


def terms_kernel(landed_ref, out_ref):
    total = landed_ref[0].astype(F32)
    for y in range(1, YH):
        total = total + landed_ref[y].astype(F32)
    wide = total.shape[1] - 4 * RANK
    total = total * (1.0 / REPLICAS)
    mean = total[:, :wide]
    left = (
        total[:, wide : wide + RANK]
        + total[:, wide + RANK : wide + 2 * RANK]
        + total[:, wide + 2 * RANK : wide + 3 * RANK]
    )
    q_terms = lax.dot_general(
        left, mean, (((0,), (0,)), ((), ())), precision=EXACT, preferred_element_type=F32
    )
    cols = wide // NEARS
    rows = left.shape[0] // 2
    folded_left = jnp.concatenate([left[:rows], left[rows:]], axis=1)
    for core in range(CORES):
        for near in range(NEARS):
            peer = near * CORES + core
            span = slice(near * cols, (near + 1) * cols)
            out_ref[peer, :HALF] = q_terms[core * HALF : (core + 1) * HALF, span]
            out_ref[peer, HALF:] = folded_left


def spread_kernel(landed_ref, out_ref, left_ref):
    core = lax.axis_index("core")
    total = landed_ref[0, :HALF]
    for peer in range(1, NEARS * CORES):
        total = total + landed_ref[peer, :HALF]

    def left_of(which):
        pieces = []
        for near in range(NEARS):
            piece = landed_ref[near * CORES + which, HALF:]
            pieces += [piece[:, :RANK], piece[:, RANK:]]
        return jnp.concatenate(pieces, axis=0)

    mine, other = left_of(core), left_of(1 - core)
    left_ref[...] = mine
    both = jnp.concatenate([mine, other], axis=0)
    gram = lax.dot_general(
        both, both, (((0,), (0,)), ((), ())), precision=EXACT, preferred_element_type=F32
    )
    own = jnp.where(core == 0, gram[:HALF], gram[HALF:])
    folded = jnp.concatenate([own[:QUARTER], own[QUARTER:]], axis=1)
    for z in range(Z):
        out_ref[z, :HALF] = total
        out_ref[z, HALF:] = folded


def factor_kernel(landed_ref, left_ref, q_ref, ortho_ref):
    sums = landed_ref[:, 0]
    for z in range(1, Z):
        sums = sums + landed_ref[:, z]
    lane = lax.broadcasted_iota(jnp.int32, (8, 2 * RANK), 1)
    sub = lax.broadcasted_iota(jnp.int32, (8, 2 * RANK), 0)
    blocks = []
    for b in range(RANK // 8):
        core, at = divmod(b, 4)
        raw = sums[core, HALF + 8 * (at % 2) : HALF + 8 * (at % 2) + 8, :]
        if at >= 2:
            raw = pltpu.roll(raw, RANK, 1)
        unit = (lane == sub + RANK + 8 * b).astype(F32)
        blocks.append(jnp.where(lane < RANK, raw, unit))

    def lane_copy(value, column):
        return jnp.broadcast_to(value[:, column : column + 1], value.shape)

    def row_copy(value, row):
        return jnp.broadcast_to(value[row : row + 1], value.shape)

    inverse_rows = []
    for b in range(RANK // 8):
        here = blocks[b]
        columns = [lane_copy(here, 8 * b + j) for j in range(8)]
        later = [
            [lane_copy(blocks[t], 8 * b + j) for j in range(8)] for t in range(b + 1, RANK // 8)
        ]
        scales = jnp.zeros_like(here)
        for j in range(8):
            pivot = row_copy(columns[j], j)
            recip = 1.0 / pivot
            scales = jnp.where(sub == j, recip, scales)
            factor = jnp.where(sub > j, columns[j] * recip, 0.0)
            here = here - factor * row_copy(here, j)
            for other in range(j + 1, 8):
                columns[other] = columns[other] - factor * row_copy(columns[other], j)
        inverse_rows.append(here * jnp.sqrt(scales))
        if b + 1 == RANK // 8:
            break
        solved = here * scales
        uppers = [columns[j] * scales for j in range(8)]
        for j in range(7, 0, -1):
            factor = jnp.where(sub < j, uppers[j], 0.0)
            solved = solved - factor * row_copy(solved, j)
        for t in range(b + 1, RANK // 8):
            update = later[t - b - 1][0] * row_copy(solved, 0)
            for j in range(1, 8):
                update = update + later[t - b - 1][j] * row_copy(solved, j)
            blocks[t] = blocks[t] - update
    inverse = jnp.concatenate(inverse_rows, axis=0)[:, RANK:]

    q_sum = jnp.concatenate([sums[0, :HALF], sums[1, :HALF]], axis=0)
    q_mine = jnp.dot(inverse, q_sum, precision=EXACT, preferred_element_type=F32).astype(BF16)
    core = lax.axis_index("core")
    q_half = jnp.where(core == 0, q_mine[:HALF], q_mine[HALF:])
    for peer in range(q_ref.shape[0]):
        q_ref[peer] = q_half
    ortho_ref[...] = lax.dot_general(
        left_ref[...],
        inverse,
        (((1,), (1,)), ((), ())),
        precision=EXACT,
        preferred_element_type=F32,
    ).astype(BF16)


def rebuild_kernel(
    q_ref, ortho_ref, merged_hbm, error_hbm, own_ref, q_next_ref, q_all, merged, error, in_sems, out_sems
):
    cols = q_ref.shape[3]
    col_count = merged.shape[1]
    wide = col_count // SPANS
    ins, outs = [], []
    for i in range(SPANS):
        span = pl.ds(i * wide, wide)
        ins.append(pltpu.make_async_copy(merged_hbm.at[:, span], merged.at[:, span], in_sems.at[i]))
        outs.append(
            pltpu.make_async_copy(error.at[:, span], error_hbm.at[0, :, span], out_sems.at[i])
        )
        ins[i].start()
    for d in range(REPLICAS):
        q_all[:HALF, d * cols : (d + 1) * cols] = q_ref[0, d]
        q_all[HALF:, d * cols : (d + 1) * cols] = q_ref[1, d]
    ortho = ortho_ref[...]
    for i in range(SPANS):
        span = slice(i * wide, (i + 1) * wide)
        approx = jnp.dot(ortho, q_all[:, span], preferred_element_type=F32)
        ins[i].wait()
        error[:, span] = (merged[:, span].astype(F32) - approx).astype(BF16)
        outs[i].start()

    own = (lax.axis_index("yh") * YL + lax.axis_index("yl")) * X + lax.axis_index("x")
    right = jnp.concatenate([q_ref[0, own], q_ref[1, own]], axis=0)
    own_ref[...] = jnp.dot(ortho, right, preferred_element_type=F32).astype(BF16)
    count = q_next_ref.shape[1] // cols
    first = (lax.axis_index("z") * CORES + lax.axis_index("core")) * count
    for i in range(count):
        q_next_ref[:HALF, i * cols : (i + 1) * cols] = q_ref[0, first + i].astype(F32)
        q_next_ref[HALF:, i * cols : (i + 1) * cols] = q_ref[1, first + i].astype(F32)
    for i in range(SPANS):
        outs[i].wait()


def rebuild(q_all, ortho, merged, shard):
    rows, col_count = merged.shape
    cols = q_all.shape[3]
    return pl.pallas_call(
        rebuild_kernel,
        out_shape=(
            shape(BF16, 1, rows, col_count),
            shape(BF16, rows, cols),
            shape(F32, RANK, shard),
        ),
        in_specs=[VMEM, VMEM, ANY],
        out_specs=[ANY, VMEM, VMEM],
        scratch_shapes=[
            pltpu.VMEM((RANK, col_count), BF16),
            pltpu.VMEM((rows, col_count), BF16),
            pltpu.VMEM((rows, col_count), BF16),
            pltpu.SemaphoreType.DMA((SPANS,)),
            pltpu.SemaphoreType.DMA((SPANS,)),
        ],
        compiler_params=pltpu.CompilerParams(vmem_limit_bytes=LIMIT),
    )(q_all, ortho, merged)


def on_device(grad, error, q_warm):
    rows, col_count = grad.shape[1:]
    cols = col_count // REPLICAS
    wide = col_count // YH
    part = rows // NEARS
    merged = merge(grad, error)

    landed = lax.all_to_all(merged.reshape(NEARS, part, col_count), NEAR, 0, 0)
    warm = lax.all_gather(q_warm.astype(BF16), FSDP, axis=1, tiled=True)
    to_far = call(left_kernel, shape(BF16, YH, part, wide + 4 * RANK), landed, warm)
    landed = lax.all_to_all(to_far, "yh", 0, 0)
    to_near = call(terms_kernel, shape(F32, NEARS * CORES, HALF + part // 2, cols), landed)
    landed = lax.all_to_all(to_near, NEAR + ("core",), 0, 0)
    terms, left = call(
        spread_kernel,
        (shape(F32, Z, HALF + QUARTER, cols), shape(F32, rows, RANK)),
        landed,
    )
    terms = lax.all_gather(lax.all_to_all(terms, "z", 0, 0), "core")
    q_copies, ortho = call(
        factor_kernel,
        (shape(BF16, REPLICAS, HALF, cols), shape(BF16, rows, RANK)),
        terms,
        left,
    )
    q_all = lax.all_gather(lax.all_to_all(q_copies, DP, 0, 0), "core")
    return rebuild(q_all, ortho, merged, q_warm.shape[1])


def solution(mesh):
    grid = Mesh(mesh.devices.reshape(YH, YL, X, Z, CORES), DP + FSDP)
    return jax.shard_map(
        on_device,
        mesh=grid,
        in_specs=(P(DP, FSDP, None), P(DP, FSDP, None), P(None, FSDP)),
        out_specs=(P(DP, FSDP, None), P(FSDP, DP), P(None, FSDP)),
        check_vma=False,
    )
```

```python
import jax
import jax.numpy as jnp
from jax import lax
from jax.experimental import pallas as pl
from jax.experimental.pallas import tpu as pltpu
from jax.sharding import Mesh, PartitionSpec as P

YH, YL, X, Z, CORES = 4, 2, 4, 8, 2
NEAR = ("yl", "x")
DP = ("yh", "yl", "x")
FSDP = ("z", "core")
NEARS = YL * X
CUTS = 4
SPANS = 4
REPLICAS = YH * YL * X
RANK = 64
HALF = RANK // 2
EXACT = lax.Precision.HIGHEST
F32, BF16 = jnp.float32, jnp.bfloat16
VMEM = pl.BlockSpec(memory_space=pltpu.VMEM)
ANY = pl.BlockSpec(memory_space=pl.ANY)
LIMIT = 32 * 1024 * 1024


def call(kernel, out, *operands):
    many = isinstance(out, (list, tuple))
    return pl.pallas_call(
        kernel,
        out_shape=out,
        in_specs=[VMEM] * len(operands),
        out_specs=[VMEM] * len(out) if many else VMEM,
        compiler_params=pltpu.CompilerParams(vmem_limit_bytes=LIMIT),
    )(*operands)


def shape(dtype, *dims):
    return jax.ShapeDtypeStruct(dims, dtype)


def merge_kernel(grad_hbm, error_hbm, merged_hbm, grad, error, merged, in_sems, out_sems):
    part = merged.shape[0] // CUTS
    copies = []
    for i in range(CUTS):
        span = pl.ds(i * part, part)
        copies.append(
            (
                pltpu.make_async_copy(grad_hbm.at[0, span], grad.at[span], in_sems.at[0, i]),
                pltpu.make_async_copy(error_hbm.at[0, span], error.at[span], in_sems.at[1, i]),
                pltpu.make_async_copy(merged.at[span], merged_hbm.at[span], out_sems.at[i]),
            )
        )
        copies[i][0].start()
        copies[i][1].start()
    for i in range(CUTS):
        copies[i][0].wait()
        copies[i][1].wait()
        span = pl.ds(i * part, part)
        merged[span] = (grad[span].astype(F32) + error[span].astype(F32)).astype(BF16)
        copies[i][2].start()
    for i in range(CUTS):
        copies[i][2].wait()


def merge(grad, error):
    _, rows, col_count = grad.shape
    return pl.pallas_call(
        merge_kernel,
        out_shape=shape(BF16, rows, col_count),
        in_specs=[ANY, ANY],
        out_specs=ANY,
        scratch_shapes=[pltpu.VMEM((rows, col_count), BF16)] * 3
        + [pltpu.SemaphoreType.DMA((2, CUTS)), pltpu.SemaphoreType.DMA((CUTS,))],
        compiler_params=pltpu.CompilerParams(vmem_limit_bytes=60 * 1024 * 1024),
    )(grad, error)


def fold(square):
    return jnp.concatenate([square[:HALF], square[HALF:]], axis=1)


def left_kernel(landed_ref, warm_ref, out_ref):
    _, rows, col_count = landed_ref.shape
    wide = col_count // YH
    stacked = landed_ref[...].reshape(NEARS * rows, col_count)
    every = lax.dot_general(
        stacked, warm_ref[...], (((1,), (1,)), ((), ())), preferred_element_type=F32
    )
    left = every[:rows]
    for peer in range(1, NEARS):
        left = left + every[peer * rows : (peer + 1) * rows]
    high = left.astype(BF16)
    rest = left - high.astype(F32)
    middle = rest.astype(BF16)
    low = (rest - middle.astype(F32)).astype(BF16)
    first = jnp.concatenate([high, middle], axis=1)
    second = jnp.concatenate([low, jnp.zeros_like(low)], axis=1)
    for y in range(YH):
        span = pl.ds(y * wide, wide)
        total = landed_ref[0, :, span].astype(F32)
        for peer in range(1, NEARS):
            total = total + landed_ref[peer, :, span].astype(F32)
        out_ref[y, :, :wide] = total.astype(BF16)
        out_ref[y, :, wide : wide + 2 * RANK] = first
        out_ref[y, :, wide + 2 * RANK :] = second


def terms_kernel(landed_ref, out_ref):
    total = landed_ref[0].astype(F32)
    for y in range(1, YH):
        total = total + landed_ref[y].astype(F32)
    wide = total.shape[1] - 4 * RANK
    total = total * (1.0 / REPLICAS)
    mean = total[:, :wide]
    left = (
        total[:, wide : wide + RANK]
        + total[:, wide + RANK : wide + 2 * RANK]
        + total[:, wide + 2 * RANK : wide + 3 * RANK]
    )
    q_terms = lax.dot_general(
        left, mean, (((0,), (0,)), ((), ())), precision=EXACT, preferred_element_type=F32
    )
    cols = wide // NEARS
    rows = left.shape[0] // 2
    folded_left = jnp.concatenate([left[:rows], left[rows:]], axis=1)
    for near in range(NEARS):
        block = q_terms[:, near * cols : (near + 1) * cols]
        for core in range(CORES):
            peer = near * CORES + core
            out_ref[peer, :HALF] = fold(block[:, core * RANK : (core + 1) * RANK])
            out_ref[peer, HALF:] = folded_left


def spread_kernel(landed_ref, out_ref, left_ref):
    core = lax.axis_index("core")
    total = landed_ref[0, :HALF]
    for peer in range(1, NEARS * CORES):
        total = total + landed_ref[peer, :HALF]

    def left_of(which):
        pieces = []
        for near in range(NEARS):
            piece = landed_ref[near * CORES + which, HALF:]
            pieces += [piece[:, :RANK], piece[:, RANK:]]
        return jnp.concatenate(pieces, axis=0)

    mine, other = left_of(core), left_of(1 - core)
    left_ref[...] = mine
    both = jnp.concatenate([mine, other], axis=0)
    gram = lax.dot_general(
        both, both, (((0,), (0,)), ((), ())), precision=EXACT, preferred_element_type=F32
    )
    folded = fold(gram)
    for z in range(Z):
        out_ref[z, :HALF] = total
        out_ref[z, HALF:] = folded


def factor_kernel(landed_ref, left_ref, q_ref, ortho_ref):
    sums = landed_ref[0]
    for z in range(1, Z):
        sums = sums + landed_ref[z]
    lane = lax.broadcasted_iota(jnp.int32, (8, 2 * RANK), 1)
    sub = lax.broadcasted_iota(jnp.int32, (8, 2 * RANK), 0)
    blocks = []
    for b in range(RANK // 8):
        at = HALF + 8 * (b % 4)
        raw = sums[at : at + 8]
        if b >= 4:
            raw = pltpu.roll(raw, RANK, 1)
        unit = (lane == sub + RANK + 8 * b).astype(F32)
        blocks.append(jnp.where(lane < RANK, raw, unit))

    def lane_copy(value, column):
        return jnp.broadcast_to(value[:, column : column + 1], value.shape)

    def row_copy(value, row):
        return jnp.broadcast_to(value[row : row + 1], value.shape)

    inverse_rows = []
    for b in range(RANK // 8):
        here = blocks[b]
        columns = [lane_copy(here, 8 * b + j) for j in range(8)]
        later = [
            [lane_copy(blocks[t], 8 * b + j) for j in range(8)] for t in range(b + 1, RANK // 8)
        ]
        scales = jnp.zeros_like(here)
        for j in range(8):
            pivot = row_copy(columns[j], j)
            recip = 1.0 / pivot
            scales = jnp.where(sub == j, recip, scales)
            factor = jnp.where(sub > j, columns[j] * recip, 0.0)
            here = here - factor * row_copy(here, j)
            for other in range(j + 1, 8):
                columns[other] = columns[other] - factor * row_copy(columns[other], j)
        inverse_rows.append(here * jnp.sqrt(scales))
        if b + 1 == RANK // 8:
            break
        solved = here * scales
        uppers = [columns[j] * scales for j in range(8)]
        for j in range(7, 0, -1):
            factor = jnp.where(sub < j, uppers[j], 0.0)
            solved = solved - factor * row_copy(solved, j)
        for t in range(b + 1, RANK // 8):
            update = later[t - b - 1][0] * row_copy(solved, 0)
            for j in range(1, 8):
                update = update + later[t - b - 1][j] * row_copy(solved, j)
            blocks[t] = blocks[t] - update
    inverse = jnp.concatenate(inverse_rows, axis=0)[:, RANK:]

    q_sum = jnp.concatenate([sums[:HALF, :RANK], sums[:HALF, RANK:]], axis=0)
    q_mine = fold(jnp.dot(inverse, q_sum, precision=EXACT, preferred_element_type=F32)).astype(BF16)
    for peer in range(q_ref.shape[0]):
        q_ref[peer] = q_mine
    ortho_ref[...] = lax.dot_general(
        left_ref[...],
        inverse,
        (((1,), (1,)), ((), ())),
        precision=EXACT,
        preferred_element_type=F32,
    ).astype(BF16)


def rebuild_kernel(
    q_ref, ortho_ref, merged, error_hbm, own_ref, q_next_ref, q_all, error, out_sems
):
    cols = q_ref.shape[3]
    col_count = merged.shape[1]
    wide = col_count // SPANS
    outs = []
    for i in range(SPANS):
        span = pl.ds(i * wide, wide)
        outs.append(
            pltpu.make_async_copy(error.at[:, span], error_hbm.at[0, :, span], out_sems.at[i])
        )
    for d in range(REPLICAS):
        first, second = q_ref[0, d], q_ref[1, d]
        span = slice(d * cols, (d + 1) * cols)
        q_all[:HALF, span] = jnp.concatenate([first[:, :RANK], second[:, :RANK]], axis=1)
        q_all[HALF:, span] = jnp.concatenate([first[:, RANK:], second[:, RANK:]], axis=1)
    ortho = ortho_ref[...]
    for i in range(SPANS):
        span = slice(i * wide, (i + 1) * wide)
        approx = jnp.dot(ortho, q_all[:, span], preferred_element_type=F32)
        error[:, span] = (merged[:, span].astype(F32) - approx).astype(BF16)
        outs[i].start()

    own = (lax.axis_index("yh") * YL + lax.axis_index("yl")) * X + lax.axis_index("x")
    right = q_all[:, pl.ds(pl.multiple_of(own * cols, cols), cols)]
    own_ref[...] = jnp.dot(ortho, right, preferred_element_type=F32).astype(BF16)
    shard = q_next_ref.shape[1]
    first = (lax.axis_index("z") * CORES + lax.axis_index("core")) * shard
    q_next_ref[...] = q_all[:, pl.ds(pl.multiple_of(first, shard), shard)].astype(F32)
    for i in range(SPANS):
        outs[i].wait()


def rebuild(q_all, ortho, merged, shard):
    rows, col_count = merged.shape
    cols = q_all.shape[3]
    return pl.pallas_call(
        rebuild_kernel,
        out_shape=(
            shape(BF16, 1, rows, col_count),
            shape(BF16, rows, cols),
            shape(F32, RANK, shard),
        ),
        in_specs=[VMEM, VMEM, VMEM],
        out_specs=[ANY, VMEM, VMEM],
        scratch_shapes=[
            pltpu.VMEM((RANK, col_count), BF16),
            pltpu.VMEM((rows, col_count), BF16),
            pltpu.SemaphoreType.DMA((SPANS,)),
        ],
        compiler_params=pltpu.CompilerParams(vmem_limit_bytes=LIMIT),
    )(q_all, ortho, merged)


def on_device(grad, error, q_warm):
    rows, col_count = grad.shape[1:]
    cols = col_count // REPLICAS
    wide = col_count // YH
    part = rows // NEARS
    merged = merge(grad, error)

    landed = lax.all_to_all(merged.reshape(NEARS, part, col_count), NEAR, 0, 0)
    warm = lax.all_gather(q_warm.astype(BF16), FSDP, axis=1, tiled=True)
    to_far = call(left_kernel, shape(BF16, YH, part, wide + 4 * RANK), landed, warm)
    landed = lax.all_to_all(to_far, "yh", 0, 0)
    to_near = call(terms_kernel, shape(F32, NEARS * CORES, HALF + part // 2, cols), landed)
    landed = lax.all_to_all(to_near, NEAR + ("core",), 0, 0)
    terms, left = call(
        spread_kernel,
        (shape(F32, Z, 2 * HALF, cols), shape(F32, rows, RANK)),
        landed,
    )
    terms = lax.all_to_all(terms, "z", 0, 0)
    q_copies, ortho = call(
        factor_kernel,
        (shape(BF16, REPLICAS, HALF, cols), shape(BF16, rows, RANK)),
        terms,
        left,
    )
    q_all = lax.all_gather(lax.all_to_all(q_copies, DP, 0, 0), "core")
    return rebuild(q_all, ortho, merged, q_warm.shape[1])


def solution(mesh):
    grid = Mesh(mesh.devices.reshape(YH, YL, X, Z, CORES), DP + FSDP)
    return jax.shard_map(
        on_device,
        mesh=grid,
        in_specs=(P(DP, FSDP, None), P(DP, FSDP, None), P(None, FSDP)),
        out_specs=(P(DP, FSDP, None), P(FSDP, DP), P(None, FSDP)),
        check_vma=False,
    )
```

```python
import jax
import jax.numpy as jnp
from jax import lax
from jax.experimental import pallas as pl
from jax.experimental.pallas import tpu as pltpu
from jax.sharding import Mesh, PartitionSpec as P

YH, YL, X, Z, CORES = 4, 2, 4, 8, 2
NEAR = ("yl", "x")
DP = ("yh", "yl", "x")
FSDP = ("z", "core")
NEARS = YL * X
CUTS = 4
SPANS = 4
REPLICAS = YH * YL * X
RANK = 64
HALF = RANK // 2
EXACT = lax.Precision.HIGHEST
F32, BF16 = jnp.float32, jnp.bfloat16
VMEM = pl.BlockSpec(memory_space=pltpu.VMEM)
ANY = pl.BlockSpec(memory_space=pl.ANY)
LIMIT = 32 * 1024 * 1024


def call(kernel, out, *operands):
    many = isinstance(out, (list, tuple))
    return pl.pallas_call(
        kernel,
        out_shape=out,
        in_specs=[VMEM] * len(operands),
        out_specs=[VMEM] * len(out) if many else VMEM,
        compiler_params=pltpu.CompilerParams(vmem_limit_bytes=LIMIT),
    )(*operands)


def shape(dtype, *dims):
    return jax.ShapeDtypeStruct(dims, dtype)


def merge_kernel(grad_hbm, error_hbm, merged_hbm, grad, error, merged, in_sems, out_sems):
    part = merged.shape[0] // CUTS
    copies = []
    for i in range(CUTS):
        span = pl.ds(i * part, part)
        copies.append(
            (
                pltpu.make_async_copy(grad_hbm.at[0, span], grad.at[span], in_sems.at[0, i]),
                pltpu.make_async_copy(error_hbm.at[0, span], error.at[span], in_sems.at[1, i]),
                pltpu.make_async_copy(merged.at[span], merged_hbm.at[span], out_sems.at[i]),
            )
        )
        copies[i][0].start()
        copies[i][1].start()
    for i in range(CUTS):
        copies[i][0].wait()
        copies[i][1].wait()
        span = pl.ds(i * part, part)
        merged[span] = (grad[span].astype(F32) + error[span].astype(F32)).astype(BF16)
        copies[i][2].start()
    for i in range(CUTS):
        copies[i][2].wait()


def merge(grad, error):
    _, rows, col_count = grad.shape
    return pl.pallas_call(
        merge_kernel,
        out_shape=shape(BF16, rows, col_count),
        in_specs=[ANY, ANY],
        out_specs=ANY,
        scratch_shapes=[pltpu.VMEM((rows, col_count), BF16)] * 3
        + [pltpu.SemaphoreType.DMA((2, CUTS)), pltpu.SemaphoreType.DMA((CUTS,))],
        compiler_params=pltpu.CompilerParams(vmem_limit_bytes=60 * 1024 * 1024),
    )(grad, error)


def fold(square):
    return jnp.concatenate([square[:HALF], square[HALF:]], axis=1)


def left_kernel(landed_ref, warm_ref, out_ref):
    near, rows, col_count = landed_ref.shape
    stacked = landed_ref[...].reshape(near * rows, col_count)
    every = lax.dot_general(
        stacked, warm_ref[...], (((1,), (1,)), ((), ())), preferred_element_type=F32
    )
    left = every[:rows]
    for n in range(1, near):
        left = left + every[n * rows : (n + 1) * rows]
    high = left.astype(BF16)
    left = jnp.concatenate([high, (left - high.astype(F32)).astype(BF16)], axis=1)
    cols = col_count // REPLICAS
    for d in range(REPLICAS):
        span = pl.ds(d * cols, cols)
        total = landed_ref[0, :, span].astype(F32)
        for n in range(1, near):
            total = total + landed_ref[n, :, span].astype(F32)
        out_ref[d, :rows] = total.astype(BF16)
        out_ref[d, rows:] = left


def mean_kernel(landed_ref, out_ref):
    rows = landed_ref.shape[1] // 2
    total = landed_ref[:NEARS].astype(F32)
    for y in range(1, YH):
        total = total + landed_ref[y * NEARS : (y + 1) * NEARS].astype(F32)
    total = total * (1.0 / REPLICAS)
    out_ref[:, :rows] = total[:, :rows]
    left = total[:, rows:, :RANK] + total[:, rows:, RANK:]
    half = rows // 2
    out_ref[:, rows:] = jnp.concatenate([left[:, :half], left[:, half:]], axis=2)


def terms_kernel(means_ref, out_ref, left_ref):
    near, rows = means_ref.shape[1], left_ref.shape[0] // NEARS
    core = lax.axis_index("core")

    def left_of(which):
        pieces = []
        for n in range(near):
            piece = means_ref[which, n, rows:]
            pieces += [piece[:, :RANK], piece[:, RANK:]]
        return jnp.concatenate(pieces, axis=0)

    def mean_of(which):
        return jnp.concatenate([means_ref[which, n, :rows] for n in range(near)], axis=0)

    mine, other = left_of(core), left_of(1 - core)
    left_ref[...] = mine
    left = jnp.concatenate([mine, other], axis=0)
    mean = jnp.concatenate([mean_of(core), mean_of(1 - core)], axis=0)
    mean = jnp.where(core == 0, mean[:, :RANK], mean[:, RANK:])
    terms = lax.dot_general(
        left,
        jnp.concatenate([left, mean], axis=1),
        (((0,), (0,)), ((), ())),
        precision=EXACT,
        preferred_element_type=F32,
    )
    for z in range(Z):
        out_ref[z] = terms


def factor_kernel(landed_ref, left_ref, q_ref, ortho_ref):
    sums = landed_ref[0]
    for z in range(1, Z):
        sums = sums + landed_ref[z]
    lane = lax.broadcasted_iota(jnp.int32, (8, 2 * RANK), 1)
    sub = lax.broadcasted_iota(jnp.int32, (8, 2 * RANK), 0)
    blocks = []
    for b in range(RANK // 8):
        unit = (lane == sub + RANK + 8 * b).astype(F32)
        blocks.append(jnp.where(lane < RANK, sums[8 * b : 8 * b + 8], unit))

    def lane_copy(value, column):
        return jnp.broadcast_to(value[:, column : column + 1], value.shape)

    def row_copy(value, row):
        return jnp.broadcast_to(value[row : row + 1], value.shape)

    inverse_rows = []
    for b in range(RANK // 8):
        here = blocks[b]
        columns = [lane_copy(here, 8 * b + j) for j in range(8)]
        later = [
            [lane_copy(blocks[t], 8 * b + j) for j in range(8)] for t in range(b + 1, RANK // 8)
        ]
        entry = [[row_copy(columns[k], i) for k in range(i + 1)] for i in range(8)]
        row = [row_copy(here, i) for i in range(8)]
        recip = [None] * 8
        factor = [[None] * 8 for _ in range(8)]
        for j in range(8):
            recip[j] = 1.0 / entry[j][j]
            for i in range(j + 1, 8):
                factor[i][j] = entry[i][j] * recip[j]
            for i in range(j + 1, 8):
                for k in range(j + 1, i + 1):
                    entry[i][k] = entry[i][k] - factor[i][j] * entry[k][j]
                row[i] = row[i] - factor[i][j] * row[j]
        done = row[0] * jnp.sqrt(recip[0])
        for i in range(1, 8):
            done = jnp.where(sub == i, row[i] * jnp.sqrt(recip[i]), done)
        inverse_rows.append(done)
        if b + 1 == RANK // 8:
            break
        solved = [row[i] * recip[i] for i in range(8)]
        for i in range(7, 0, -1):
            for j in range(i):
                solved[j] = solved[j] - factor[i][j] * solved[i]
        for t in range(b + 1, RANK // 8):
            update = later[t - b - 1][0] * solved[0]
            for j in range(1, 8):
                update = update + later[t - b - 1][j] * solved[j]
            blocks[t] = blocks[t] - update
    inverse = jnp.concatenate(inverse_rows, axis=0)[:, RANK:]

    q_sum = sums[:, RANK:]
    q_mine = fold(jnp.dot(inverse, q_sum, precision=EXACT, preferred_element_type=F32)).astype(BF16)
    for peer in range(q_ref.shape[0]):
        q_ref[peer] = q_mine
    ortho_ref[...] = lax.dot_general(
        left_ref[...],
        inverse,
        (((1,), (1,)), ((), ())),
        precision=EXACT,
        preferred_element_type=F32,
    ).astype(BF16)


def rebuild_kernel(
    q_ref, ortho_ref, merged, error_hbm, own_ref, q_next_ref, q_all, error, out_sems
):
    cols = q_ref.shape[3]
    col_count = merged.shape[1]
    wide = col_count // SPANS
    outs = []
    for i in range(SPANS):
        span = pl.ds(i * wide, wide)
        outs.append(
            pltpu.make_async_copy(error.at[:, span], error_hbm.at[0, :, span], out_sems.at[i])
        )
    ortho = ortho_ref[...]
    for i in range(SPANS):
        span = slice(i * wide, (i + 1) * wide)
        for d in range(i * wide // cols, (i + 1) * wide // cols):
            first, second = q_ref[0, d], q_ref[1, d]
            block = slice(d * cols, (d + 1) * cols)
            q_all[:HALF, block] = jnp.concatenate([first[:, :RANK], second[:, :RANK]], axis=1)
            q_all[HALF:, block] = jnp.concatenate([first[:, RANK:], second[:, RANK:]], axis=1)
        approx = jnp.dot(ortho, q_all[:, span], preferred_element_type=F32)
        error[:, span] = (merged[:, span].astype(F32) - approx).astype(BF16)
        outs[i].start()

    own = (lax.axis_index("yh") * YL + lax.axis_index("yl")) * X + lax.axis_index("x")
    right = q_all[:, pl.ds(pl.multiple_of(own * cols, cols), cols)]
    own_ref[...] = jnp.dot(ortho, right, preferred_element_type=F32).astype(BF16)
    shard = q_next_ref.shape[1]
    first = (lax.axis_index("z") * CORES + lax.axis_index("core")) * shard
    q_next_ref[...] = q_all[:, pl.ds(pl.multiple_of(first, shard), shard)].astype(F32)
    for i in range(SPANS):
        outs[i].wait()


def rebuild(q_all, ortho, merged, shard):
    rows, col_count = merged.shape
    cols = q_all.shape[3]
    return pl.pallas_call(
        rebuild_kernel,
        out_shape=(
            shape(BF16, 1, rows, col_count),
            shape(BF16, rows, cols),
            shape(F32, RANK, shard),
        ),
        in_specs=[VMEM, VMEM, VMEM],
        out_specs=[ANY, VMEM, VMEM],
        scratch_shapes=[
            pltpu.VMEM((RANK, col_count), BF16),
            pltpu.VMEM((rows, col_count), BF16),
            pltpu.SemaphoreType.DMA((SPANS,)),
        ],
        compiler_params=pltpu.CompilerParams(vmem_limit_bytes=LIMIT),
    )(q_all, ortho, merged)


def on_device(grad, error, q_warm):
    rows, col_count = grad.shape[1:]
    cols = col_count // REPLICAS
    part = rows // NEARS
    merged = merge(grad, error)

    landed = lax.all_to_all(merged.reshape(NEARS, part, col_count), NEAR, 0, 0)
    warm = lax.all_gather(q_warm.astype(BF16), FSDP, axis=1, tiled=True)
    shares = call(left_kernel, shape(BF16, REPLICAS, 2 * part, cols), landed, warm)
    shares = lax.all_to_all(shares, DP, 0, 0)
    means = call(mean_kernel, shape(F32, NEARS, part + part // 2, cols), shares)
    terms, left = call(
        terms_kernel,
        (shape(F32, Z, RANK, 2 * RANK), shape(F32, rows, RANK)),
        lax.all_gather(means, "core"),
    )
    terms = lax.all_to_all(terms, "z", 0, 0)
    q_copies, ortho = call(
        factor_kernel,
        (shape(BF16, REPLICAS, HALF, cols), shape(BF16, rows, RANK)),
        terms,
        left,
    )
    q_all = lax.all_gather(lax.all_to_all(q_copies, DP, 0, 0), "core")
    return rebuild(q_all, ortho, merged, q_warm.shape[1])


def solution(mesh):
    grid = Mesh(mesh.devices.reshape(YH, YL, X, Z, CORES), DP + FSDP)
    return jax.shard_map(
        on_device,
        mesh=grid,
        in_specs=(P(DP, FSDP, None), P(DP, FSDP, None), P(None, FSDP)),
        out_specs=(P(DP, FSDP, None), P(FSDP, DP), P(None, FSDP)),
        check_vma=False,
    )
```

```python
import jax
import jax.numpy as jnp
from jax import lax
from jax.experimental import pallas as pl
from jax.experimental.pallas import tpu as pltpu
from jax.sharding import Mesh, PartitionSpec as P

YH, YL, X, Z, CORES = 4, 2, 4, 8, 2
NEAR = ("yl", "x")
DP = ("yh", "yl", "x")
FSDP = ("z", "core")
NEARS = YL * X
CUTS = 4
SPANS = 4
REPLICAS = YH * YL * X
RANK = 64
HALF = RANK // 2
EXACT = lax.Precision.HIGHEST
F32, BF16 = jnp.float32, jnp.bfloat16
VMEM = pl.BlockSpec(memory_space=pltpu.VMEM)
ANY = pl.BlockSpec(memory_space=pl.ANY)
LIMIT = 32 * 1024 * 1024


def call(kernel, out, *operands, scratch=()):
    many = isinstance(out, (list, tuple))
    return pl.pallas_call(
        kernel,
        out_shape=out,
        in_specs=[VMEM] * len(operands),
        out_specs=[VMEM] * len(out) if many else VMEM,
        scratch_shapes=list(scratch),
        compiler_params=pltpu.CompilerParams(vmem_limit_bytes=LIMIT),
    )(*operands)


def shape(dtype, *dims):
    return jax.ShapeDtypeStruct(dims, dtype)


def merge_kernel(grad_hbm, error_hbm, merged_hbm, grad, error, merged, in_sems, out_sems):
    part = merged.shape[0] // CUTS
    copies = []
    for i in range(CUTS):
        span = pl.ds(i * part, part)
        copies.append(
            (
                pltpu.make_async_copy(grad_hbm.at[0, span], grad.at[span], in_sems.at[0, i]),
                pltpu.make_async_copy(error_hbm.at[0, span], error.at[span], in_sems.at[1, i]),
                pltpu.make_async_copy(merged.at[span], merged_hbm.at[span], out_sems.at[i]),
            )
        )
        copies[i][0].start()
        copies[i][1].start()
    for i in range(CUTS):
        copies[i][0].wait()
        copies[i][1].wait()
        span = pl.ds(i * part, part)
        merged[span] = (grad[span].astype(F32) + error[span].astype(F32)).astype(BF16)
        copies[i][2].start()
    for i in range(CUTS):
        copies[i][2].wait()


def merge(grad, error):
    _, rows, col_count = grad.shape
    return pl.pallas_call(
        merge_kernel,
        out_shape=shape(BF16, rows, col_count),
        in_specs=[ANY, ANY],
        out_specs=ANY,
        scratch_shapes=[pltpu.VMEM((rows, col_count), BF16)] * 3
        + [pltpu.SemaphoreType.DMA((2, CUTS)), pltpu.SemaphoreType.DMA((CUTS,))],
        compiler_params=pltpu.CompilerParams(vmem_limit_bytes=60 * 1024 * 1024),
    )(grad, error)


def fold(square):
    return jnp.concatenate([square[:HALF], square[HALF:]], axis=1)


def left_kernel(landed_ref, warm_ref, out_ref):
    near, rows, col_count = landed_ref.shape
    stacked = landed_ref[...].reshape(near * rows, col_count)
    every = lax.dot_general(
        stacked, warm_ref[...], (((1,), (1,)), ((), ())), preferred_element_type=F32
    )
    left = every[:rows]
    for n in range(1, near):
        left = left + every[n * rows : (n + 1) * rows]
    high = left.astype(BF16)
    left = jnp.concatenate([high, (left - high.astype(F32)).astype(BF16)], axis=1)
    cols = col_count // REPLICAS
    for d in range(REPLICAS):
        span = pl.ds(d * cols, cols)
        total = landed_ref[0, :, span].astype(F32)
        for n in range(1, near):
            total = total + landed_ref[n, :, span].astype(F32)
        out_ref[d, :rows] = total.astype(BF16)
        out_ref[d, rows:] = left


def mean_kernel(landed_ref, out_ref):
    rows = landed_ref.shape[1] // 2
    total = landed_ref[:NEARS].astype(F32)
    for y in range(1, YH):
        total = total + landed_ref[y * NEARS : (y + 1) * NEARS].astype(F32)
    total = total * (1.0 / REPLICAS)
    out_ref[:, :rows] = total[:, :rows]
    left = total[:, rows:, :RANK] + total[:, rows:, RANK:]
    half = rows // 2
    out_ref[:, rows:] = jnp.concatenate([left[:, :half], left[:, half:]], axis=2)


def terms_kernel(means_ref, out_ref, left_ref):
    near, rows = means_ref.shape[1], left_ref.shape[0] // NEARS
    core = lax.axis_index("core")

    def left_of(which):
        pieces = []
        for n in range(near):
            piece = means_ref[which, n, rows:]
            pieces += [piece[:, :RANK], piece[:, RANK:]]
        return jnp.concatenate(pieces, axis=0)

    def mean_of(which):
        return jnp.concatenate([means_ref[which, n, :rows] for n in range(near)], axis=0)

    mine, other = left_of(core), left_of(1 - core)
    left_ref[...] = mine
    left = jnp.concatenate([mine, other], axis=0)
    mean = jnp.concatenate([mean_of(core), mean_of(1 - core)], axis=0)
    mean = jnp.where(core == 0, mean[:, :RANK], mean[:, RANK:])
    terms = lax.dot_general(
        left,
        jnp.concatenate([left, mean], axis=1),
        (((0,), (0,)), ((), ())),
        precision=EXACT,
        preferred_element_type=F32,
    )
    for z in range(Z):
        out_ref[z] = terms


def factor_kernel(landed_ref, left_ref, q_ref, ortho_ref, held):
    sums = landed_ref[0]
    for z in range(1, Z):
        sums = sums + landed_ref[z]
    lane = lax.broadcasted_iota(jnp.int32, (8, 2 * RANK), 1)
    sub = lax.broadcasted_iota(jnp.int32, (8, 2 * RANK), 0)
    blocks = []
    for b in range(RANK // 8):
        unit = (lane == sub + RANK + 8 * b).astype(F32)
        blocks.append(jnp.where(lane < RANK, sums[8 * b : 8 * b + 8], unit))

    def lane_copy(value, column):
        return jnp.broadcast_to(value[:, column : column + 1], value.shape)

    def row_copy(slot, row):
        return jnp.broadcast_to(held[slot, row : row + 1, :], (8, 2 * RANK))

    inverse_rows = []
    for b in range(RANK // 8):
        here = blocks[b]
        columns = [lane_copy(here, 8 * b + j) for j in range(8)]
        later = [
            [lane_copy(blocks[t], 8 * b + j) for j in range(8)] for t in range(b + 1, RANK // 8)
        ]
        base = 9 * (b % 2)
        held[base + 8] = here
        for k in range(8):
            held[base + k] = columns[k]
        entry = [[row_copy(base + k, i) for k in range(i + 1)] for i in range(8)]
        row = [row_copy(base + 8, i) for i in range(8)]
        recip = [None] * 8
        factor = [[None] * 8 for _ in range(8)]
        for j in range(8):
            recip[j] = 1.0 / entry[j][j]
            for i in range(j + 1, 8):
                factor[i][j] = entry[i][j] * recip[j]
            for i in range(j + 1, 8):
                for k in range(j + 1, i + 1):
                    entry[i][k] = entry[i][k] - factor[i][j] * entry[k][j]
                row[i] = row[i] - factor[i][j] * row[j]
        done = row[0] * jnp.sqrt(recip[0])
        for i in range(1, 8):
            done = jnp.where(sub == i, row[i] * jnp.sqrt(recip[i]), done)
        inverse_rows.append(done)
        if b + 1 == RANK // 8:
            break
        solved = [row[i] * recip[i] for i in range(8)]
        for i in range(7, 0, -1):
            for j in range(i):
                solved[j] = solved[j] - factor[i][j] * solved[i]
        for t in range(b + 1, RANK // 8):
            update = later[t - b - 1][0] * solved[0]
            for j in range(1, 8):
                update = update + later[t - b - 1][j] * solved[j]
            blocks[t] = blocks[t] - update
    inverse = jnp.concatenate(inverse_rows, axis=0)[:, RANK:]

    q_sum = sums[:, RANK:]
    q_mine = jnp.dot(inverse, q_sum, precision=EXACT, preferred_element_type=F32).astype(BF16)
    upper, lower = q_mine[:HALF], q_mine[HALF:]
    q_mine = jnp.where(
        lax.axis_index("core") == 0,
        jnp.concatenate([upper, lower], axis=1),
        jnp.concatenate([lower, upper], axis=1),
    )
    for peer in range(q_ref.shape[0]):
        q_ref[peer] = q_mine
    ortho_ref[...] = lax.dot_general(
        left_ref[...],
        inverse,
        (((1,), (1,)), ((), ())),
        precision=EXACT,
        preferred_element_type=F32,
    ).astype(BF16)


def rebuild_kernel(
    q_ref, ortho_ref, merged, error_hbm, own_ref, q_next_ref, q_all, error, out_sems
):
    cols = q_ref.shape[3]
    col_count = merged.shape[1]
    wide = col_count // SPANS
    outs = []
    for i in range(SPANS):
        span = pl.ds(i * wide, wide)
        outs.append(
            pltpu.make_async_copy(error.at[:, span], error_hbm.at[0, :, span], out_sems.at[i])
        )
    ortho = ortho_ref[...]
    lane = lax.broadcasted_iota(jnp.int32, (HALF, cols), 1)
    for i in range(SPANS):
        span = slice(i * wide, (i + 1) * wide)
        for d in range(i * wide // cols, (i + 1) * wide // cols):
            first, second = q_ref[0, d], q_ref[1, d]
            block = slice(d * cols, (d + 1) * cols)
            q_all[:HALF, block] = jnp.where(lane < RANK, first, second)
            mixed = jnp.where(lane < RANK, second, first)
            q_all[HALF:, block] = jnp.concatenate([mixed[:, RANK:], mixed[:, :RANK]], axis=1)
        approx = jnp.dot(ortho, q_all[:, span], preferred_element_type=F32)
        error[:, span] = (merged[:, span].astype(F32) - approx).astype(BF16)
        outs[i].start()

    own = (lax.axis_index("yh") * YL + lax.axis_index("yl")) * X + lax.axis_index("x")
    right = q_all[:, pl.ds(pl.multiple_of(own * cols, cols), cols)]
    own_ref[...] = jnp.dot(ortho, right, preferred_element_type=F32).astype(BF16)
    shard = q_next_ref.shape[1]
    first = (lax.axis_index("z") * CORES + lax.axis_index("core")) * shard
    q_next_ref[...] = q_all[:, pl.ds(pl.multiple_of(first, shard), shard)].astype(F32)
    for i in range(SPANS):
        outs[i].wait()


def rebuild(q_all, ortho, merged, shard):
    rows, col_count = merged.shape
    cols = q_all.shape[3]
    return pl.pallas_call(
        rebuild_kernel,
        out_shape=(
            shape(BF16, 1, rows, col_count),
            shape(BF16, rows, cols),
            shape(F32, RANK, shard),
        ),
        in_specs=[VMEM, VMEM, VMEM],
        out_specs=[ANY, VMEM, VMEM],
        scratch_shapes=[
            pltpu.VMEM((RANK, col_count), BF16),
            pltpu.VMEM((rows, col_count), BF16),
            pltpu.SemaphoreType.DMA((SPANS,)),
        ],
        compiler_params=pltpu.CompilerParams(vmem_limit_bytes=LIMIT),
    )(q_all, ortho, merged)


def on_device(grad, error, q_warm):
    rows, col_count = grad.shape[1:]
    cols = col_count // REPLICAS
    part = rows // NEARS
    merged = merge(grad, error)

    landed = lax.all_to_all(merged.reshape(NEARS, part, col_count), NEAR, 0, 0)
    warm = lax.all_gather(q_warm.astype(BF16), FSDP, axis=1, tiled=True)
    shares = call(left_kernel, shape(BF16, REPLICAS, 2 * part, cols), landed, warm)
    shares = lax.all_to_all(shares, DP, 0, 0)
    means = call(mean_kernel, shape(F32, NEARS, part + part // 2, cols), shares)
    terms, left = call(
        terms_kernel,
        (shape(F32, Z, RANK, 2 * RANK), shape(F32, rows, RANK)),
        lax.all_gather(means, "core"),
    )
    terms = lax.all_to_all(terms, "z", 0, 0)
    q_copies, ortho = call(
        factor_kernel,
        (shape(BF16, REPLICAS, HALF, cols), shape(BF16, rows, RANK)),
        terms,
        left,
        scratch=[pltpu.VMEM((18, 8, 2 * RANK), F32)],
    )
    q_all = lax.all_gather(lax.all_to_all(q_copies, DP, 0, 0), "core")
    return rebuild(q_all, ortho, merged, q_warm.shape[1])


def solution(mesh):
    grid = Mesh(mesh.devices.reshape(YH, YL, X, Z, CORES), DP + FSDP)
    return jax.shard_map(
        on_device,
        mesh=grid,
        in_specs=(P(DP, FSDP, None), P(DP, FSDP, None), P(None, FSDP)),
        out_specs=(P(DP, FSDP, None), P(FSDP, DP), P(None, FSDP)),
        check_vma=False,
    )
```

```python
import jax
import jax.numpy as jnp
from jax import lax
from jax.experimental import pallas as pl
from jax.experimental.pallas import tpu as pltpu
from jax.sharding import Mesh, PartitionSpec as P

YH, YL, X, Z, CORES = 4, 2, 4, 8, 2
NEAR = ("yl", "x")
DP = ("yh", "yl", "x")
FSDP = ("z", "core")
NEARS = YL * X
CUTS = 4
SPANS = 4
REPLICAS = YH * YL * X
RANK = 64
HALF = RANK // 2
EXACT = lax.Precision.HIGHEST
F32, BF16 = jnp.float32, jnp.bfloat16
VMEM = pl.BlockSpec(memory_space=pltpu.VMEM)
ANY = pl.BlockSpec(memory_space=pl.ANY)
LIMIT = 32 * 1024 * 1024


def call(kernel, out, *operands, scratch=()):
    many = isinstance(out, (list, tuple))
    return pl.pallas_call(
        kernel,
        out_shape=out,
        in_specs=[VMEM] * len(operands),
        out_specs=[VMEM] * len(out) if many else VMEM,
        scratch_shapes=list(scratch),
        compiler_params=pltpu.CompilerParams(vmem_limit_bytes=LIMIT),
    )(*operands)


def shape(dtype, *dims):
    return jax.ShapeDtypeStruct(dims, dtype)


def merge_kernel(grad_hbm, error_hbm, merged_hbm, grad, error, merged, in_sems, out_sems):
    part = merged.shape[0] // CUTS
    copies = []
    for i in range(CUTS):
        span = pl.ds(i * part, part)
        copies.append(
            (
                pltpu.make_async_copy(grad_hbm.at[0, span], grad.at[span], in_sems.at[0, i]),
                pltpu.make_async_copy(error_hbm.at[0, span], error.at[span], in_sems.at[1, i]),
                pltpu.make_async_copy(merged.at[span], merged_hbm.at[span], out_sems.at[i]),
            )
        )
        copies[i][0].start()
        copies[i][1].start()
    for i in range(CUTS):
        copies[i][0].wait()
        copies[i][1].wait()
        span = pl.ds(i * part, part)
        merged[span] = (grad[span].astype(F32) + error[span].astype(F32)).astype(BF16)
        copies[i][2].start()
    for i in range(CUTS):
        copies[i][2].wait()


def merge(grad, error):
    _, rows, col_count = grad.shape
    return pl.pallas_call(
        merge_kernel,
        out_shape=shape(BF16, rows, col_count),
        in_specs=[ANY, ANY],
        out_specs=ANY,
        scratch_shapes=[pltpu.VMEM((rows, col_count), BF16)] * 3
        + [pltpu.SemaphoreType.DMA((2, CUTS)), pltpu.SemaphoreType.DMA((CUTS,))],
        compiler_params=pltpu.CompilerParams(vmem_limit_bytes=60 * 1024 * 1024),
    )(grad, error)


def fold(square):
    return jnp.concatenate([square[:HALF], square[HALF:]], axis=1)


def left_kernel(landed_ref, warm_ref, out_ref):
    near, rows, col_count = landed_ref.shape
    stacked = landed_ref[...].reshape(near * rows, col_count)
    every = lax.dot_general(
        stacked, warm_ref[...], (((1,), (1,)), ((), ())), preferred_element_type=F32
    )
    left = every[:rows]
    for n in range(1, near):
        left = left + every[n * rows : (n + 1) * rows]
    high = left.astype(BF16)
    left = jnp.concatenate([high, (left - high.astype(F32)).astype(BF16)], axis=1)
    cols = col_count // REPLICAS
    for d in range(REPLICAS):
        span = pl.ds(d * cols, cols)
        total = landed_ref[0, :, span].astype(F32)
        for n in range(1, near):
            total = total + landed_ref[n, :, span].astype(F32)
        out_ref[d, :rows] = total.astype(BF16)
        out_ref[d, rows:] = left


def mean_kernel(landed_ref, out_ref):
    rows = landed_ref.shape[1] // 2
    total = landed_ref[:NEARS].astype(F32)
    for y in range(1, YH):
        total = total + landed_ref[y * NEARS : (y + 1) * NEARS].astype(F32)
    total = total * (1.0 / REPLICAS)
    out_ref[:, :rows] = total[:, :rows]
    left = total[:, rows:, :RANK] + total[:, rows:, RANK:]
    half = rows // 2
    out_ref[:, rows:] = jnp.concatenate([left[:, :half], left[:, half:]], axis=2)


def terms_kernel(means_ref, out_ref, left_ref):
    near, rows = means_ref.shape[1], left_ref.shape[0] // NEARS
    core = lax.axis_index("core")

    def left_of(which):
        pieces = []
        for n in range(near):
            piece = means_ref[which, n, rows:]
            pieces += [piece[:, :RANK], piece[:, RANK:]]
        return jnp.concatenate(pieces, axis=0)

    def mean_of(which):
        return jnp.concatenate([means_ref[which, n, :rows] for n in range(near)], axis=0)

    mine, other = left_of(core), left_of(1 - core)
    left_ref[...] = mine
    left = jnp.concatenate([mine, other], axis=0)
    mean = jnp.concatenate([mean_of(core), mean_of(1 - core)], axis=0)
    mean = jnp.where(core == 0, mean[:, :RANK], mean[:, RANK:])
    terms = lax.dot_general(
        left,
        jnp.concatenate([left, mean], axis=1),
        (((0,), (0,)), ((), ())),
        precision=EXACT,
        preferred_element_type=F32,
    )
    for z in range(Z):
        out_ref[z] = terms


def factor_kernel(landed_ref, left_ref, q_ref, ortho_ref, held):
    sums = landed_ref[0]
    for z in range(1, Z):
        sums = sums + landed_ref[z]
    lane = lax.broadcasted_iota(jnp.int32, (8, 2 * RANK), 1)
    sub = lax.broadcasted_iota(jnp.int32, (8, 2 * RANK), 0)
    blocks = []
    for b in range(RANK // 8):
        unit = (lane == sub + RANK + 8 * b).astype(F32)
        blocks.append(jnp.where(lane < RANK, sums[8 * b : 8 * b + 8], unit))

    def lane_copy(value, column):
        return jnp.broadcast_to(value[:, column : column + 1], value.shape)

    def row_copy(slot, row):
        return jnp.broadcast_to(held[slot, row : row + 1, :], (8, 2 * RANK))

    inverse_rows = []
    for b in range(RANK // 8):
        here = blocks[b]
        columns = [lane_copy(here, 8 * b + j) for j in range(8)]
        later = [
            [lane_copy(blocks[t], 8 * b + j) for j in range(8)] for t in range(b + 1, RANK // 8)
        ]
        base = 9 * (b % 2)
        held[base + 8] = here
        for k in range(8):
            held[base + k] = columns[k]
        entry = [[row_copy(base + k, i) for k in range(i + 1)] for i in range(8)]
        row = [row_copy(base + 8, i) for i in range(8)]
        recip = [None] * 8
        factor = [[None] * 8 for _ in range(8)]
        for j in range(8):
            recip[j] = 1.0 / entry[j][j]
            for i in range(j + 1, 8):
                factor[i][j] = entry[i][j] * recip[j]
            for i in range(j + 1, 8):
                for k in range(j + 1, i + 1):
                    entry[i][k] = entry[i][k] - factor[i][j] * entry[k][j]
                row[i] = row[i] - factor[i][j] * row[j]
        done = row[0] * jnp.sqrt(recip[0])
        for i in range(1, 8):
            done = jnp.where(sub == i, row[i] * jnp.sqrt(recip[i]), done)
        inverse_rows.append(done)
        if b + 1 == RANK // 8:
            break
        solved = [row[i] * recip[i] for i in range(8)]
        for i in range(7, 0, -1):
            for j in range(i):
                solved[j] = solved[j] - factor[i][j] * solved[i]
        for t in range(b + 1, RANK // 8):
            update = later[t - b - 1][0] * solved[0]
            for j in range(1, 8):
                update = update + later[t - b - 1][j] * solved[j]
            blocks[t] = blocks[t] - update
    inverse = jnp.concatenate(inverse_rows, axis=0)[:, RANK:]

    q_sum = sums[:, RANK:]
    q_mine = jnp.dot(inverse, q_sum, precision=EXACT, preferred_element_type=F32).astype(BF16)
    upper, lower = q_mine[:HALF], q_mine[HALF:]
    q_mine = jnp.where(
        lax.axis_index("core") == 0,
        jnp.concatenate([upper, lower], axis=1),
        jnp.concatenate([lower, upper], axis=1),
    )
    for peer in range(q_ref.shape[0]):
        q_ref[peer] = q_mine
    ortho_ref[...] = lax.dot_general(
        left_ref[...],
        inverse,
        (((1,), (1,)), ((), ())),
        precision=EXACT,
        preferred_element_type=F32,
    ).astype(BF16)


def rebuild_kernel(
    q_ref,
    ortho_ref,
    merged,
    error_hbm,
    own_hbm,
    q_next_hbm,
    q_all,
    error,
    own,
    q_next,
    out_sems,
    small_sems,
):
    cols = q_ref.shape[3]
    col_count = merged.shape[1]
    wide = col_count // SPANS
    outs = []
    for i in range(SPANS):
        span = pl.ds(i * wide, wide)
        outs.append(
            pltpu.make_async_copy(error.at[:, span], error_hbm.at[0, :, span], out_sems.at[i])
        )
    ortho = ortho_ref[...]
    lane = lax.broadcasted_iota(jnp.int32, (HALF, cols), 1)

    def upper_of(d):
        return jnp.where(lane < RANK, q_ref[0, d], q_ref[1, d])

    def lower_of(d):
        mixed = jnp.where(lane < RANK, q_ref[1, d], q_ref[0, d])
        return jnp.concatenate([mixed[:, RANK:], mixed[:, :RANK]], axis=1)

    mine = (lax.axis_index("yh") * YL + lax.axis_index("yl")) * X + lax.axis_index("x")
    right = jnp.concatenate([upper_of(mine), lower_of(mine)], axis=0)
    own[...] = jnp.dot(ortho, right, preferred_element_type=F32).astype(BF16)
    own_copy = pltpu.make_async_copy(own, own_hbm, small_sems.at[0])
    own_copy.start()
    count = q_next.shape[1] // cols
    first = (lax.axis_index("z") * CORES + lax.axis_index("core")) * count
    for i in range(count):
        q_next[:HALF, i * cols : (i + 1) * cols] = upper_of(first + i).astype(F32)
        q_next[HALF:, i * cols : (i + 1) * cols] = lower_of(first + i).astype(F32)
    q_next_copy = pltpu.make_async_copy(q_next, q_next_hbm, small_sems.at[1])
    q_next_copy.start()

    for i in range(SPANS):
        span = slice(i * wide, (i + 1) * wide)
        for d in range(i * wide // cols, (i + 1) * wide // cols):
            block = slice(d * cols, (d + 1) * cols)
            q_all[:HALF, block] = upper_of(d)
            q_all[HALF:, block] = lower_of(d)
        approx = jnp.dot(ortho, q_all[:, span], preferred_element_type=F32)
        error[:, span] = (merged[:, span].astype(F32) - approx).astype(BF16)
        outs[i].start()
    own_copy.wait()
    q_next_copy.wait()
    for i in range(SPANS):
        outs[i].wait()


def rebuild(q_all, ortho, merged, shard):
    rows, col_count = merged.shape
    cols = q_all.shape[3]
    return pl.pallas_call(
        rebuild_kernel,
        out_shape=(
            shape(BF16, 1, rows, col_count),
            shape(BF16, rows, cols),
            shape(F32, RANK, shard),
        ),
        in_specs=[VMEM, VMEM, VMEM],
        out_specs=[ANY, ANY, ANY],
        scratch_shapes=[
            pltpu.VMEM((RANK, col_count), BF16),
            pltpu.VMEM((rows, col_count), BF16),
            pltpu.VMEM((rows, cols), BF16),
            pltpu.VMEM((RANK, shard), F32),
            pltpu.SemaphoreType.DMA((SPANS,)),
            pltpu.SemaphoreType.DMA((2,)),
        ],
        compiler_params=pltpu.CompilerParams(vmem_limit_bytes=LIMIT),
    )(q_all, ortho, merged)


def on_device(grad, error, q_warm):
    rows, col_count = grad.shape[1:]
    cols = col_count // REPLICAS
    part = rows // NEARS
    merged = merge(grad, error)

    landed = lax.all_to_all(merged.reshape(NEARS, part, col_count), NEAR, 0, 0)
    warm = lax.all_gather(q_warm.astype(BF16), FSDP, axis=1, tiled=True)
    shares = call(left_kernel, shape(BF16, REPLICAS, 2 * part, cols), landed, warm)
    shares = lax.all_to_all(shares, DP, 0, 0)
    means = call(mean_kernel, shape(F32, NEARS, part + part // 2, cols), shares)
    terms, left = call(
        terms_kernel,
        (shape(F32, Z, RANK, 2 * RANK), shape(F32, rows, RANK)),
        lax.all_gather(means, "core"),
    )
    terms = lax.all_to_all(terms, "z", 0, 0)
    q_copies, ortho = call(
        factor_kernel,
        (shape(BF16, REPLICAS, HALF, cols), shape(BF16, rows, RANK)),
        terms,
        left,
        scratch=[pltpu.VMEM((18, 8, 2 * RANK), F32)],
    )
    q_all = lax.all_gather(lax.all_to_all(q_copies, DP, 0, 0), "core")
    return rebuild(q_all, ortho, merged, q_warm.shape[1])


def solution(mesh):
    grid = Mesh(mesh.devices.reshape(YH, YL, X, Z, CORES), DP + FSDP)
    return jax.shard_map(
        on_device,
        mesh=grid,
        in_specs=(P(DP, FSDP, None), P(DP, FSDP, None), P(None, FSDP)),
        out_specs=(P(DP, FSDP, None), P(FSDP, DP), P(None, FSDP)),
        check_vma=False,
    )
```

```python
import jax
import jax.numpy as jnp
from jax import lax
from jax.experimental import pallas as pl
from jax.experimental.pallas import tpu as pltpu
from jax.sharding import Mesh, PartitionSpec as P

YH, YL, X, Z, CORES = 4, 2, 4, 8, 2
NEAR = ("yl", "x")
DP = ("yh", "yl", "x")
FSDP = ("z", "core")
NEARS = YL * X
CUTS = 4
SPANS = 4
REPLICAS = YH * YL * X
RANK = 64
HALF = RANK // 2
EXACT = lax.Precision.HIGHEST
F32, BF16 = jnp.float32, jnp.bfloat16
VMEM = pl.BlockSpec(memory_space=pltpu.VMEM)
ANY = pl.BlockSpec(memory_space=pl.ANY)
LIMIT = 32 * 1024 * 1024


def call(kernel, out, *operands, scratch=()):
    many = isinstance(out, (list, tuple))
    return pl.pallas_call(
        kernel,
        out_shape=out,
        in_specs=[VMEM] * len(operands),
        out_specs=[VMEM] * len(out) if many else VMEM,
        scratch_shapes=list(scratch),
        compiler_params=pltpu.CompilerParams(vmem_limit_bytes=LIMIT),
    )(*operands)


def shape(dtype, *dims):
    return jax.ShapeDtypeStruct(dims, dtype)


def merge_kernel(grad_hbm, error_hbm, merged_hbm, grad, error, merged, in_sems, out_sems):
    part = merged.shape[0] // CUTS
    copies = []
    for i in range(CUTS):
        span = pl.ds(i * part, part)
        copies.append(
            (
                pltpu.make_async_copy(grad_hbm.at[0, span], grad.at[span], in_sems.at[0, i]),
                pltpu.make_async_copy(error_hbm.at[0, span], error.at[span], in_sems.at[1, i]),
                pltpu.make_async_copy(merged.at[span], merged_hbm.at[span], out_sems.at[i]),
            )
        )
        copies[i][0].start()
        copies[i][1].start()
    for i in range(CUTS):
        copies[i][0].wait()
        copies[i][1].wait()
        span = pl.ds(i * part, part)
        merged[span] = (grad[span].astype(F32) + error[span].astype(F32)).astype(BF16)
        copies[i][2].start()
    for i in range(CUTS):
        copies[i][2].wait()


def merge(grad, error):
    _, rows, col_count = grad.shape
    return pl.pallas_call(
        merge_kernel,
        out_shape=shape(BF16, rows, col_count),
        in_specs=[ANY, ANY],
        out_specs=ANY,
        scratch_shapes=[pltpu.VMEM((rows, col_count), BF16)] * 3
        + [pltpu.SemaphoreType.DMA((2, CUTS)), pltpu.SemaphoreType.DMA((CUTS,))],
        compiler_params=pltpu.CompilerParams(vmem_limit_bytes=60 * 1024 * 1024),
    )(grad, error)


def fold(square):
    return jnp.concatenate([square[:HALF], square[HALF:]], axis=1)


def left_kernel(landed_ref, warm_ref, out_ref):
    near, rows, col_count = landed_ref.shape
    stacked = landed_ref[...].reshape(near * rows, col_count)
    every = lax.dot_general(
        stacked, warm_ref[...], (((1,), (1,)), ((), ())), preferred_element_type=F32
    )
    left = every[:rows]
    for n in range(1, near):
        left = left + every[n * rows : (n + 1) * rows]
    high = left.astype(BF16)
    left = jnp.concatenate([high, (left - high.astype(F32)).astype(BF16)], axis=1)
    cols = col_count // REPLICAS
    for d in range(REPLICAS):
        span = pl.ds(d * cols, cols)
        total = landed_ref[0, :, span].astype(F32)
        for n in range(1, near):
            total = total + landed_ref[n, :, span].astype(F32)
        out_ref[d, :rows] = total.astype(BF16)
        out_ref[d, rows:] = left


def mean_kernel(landed_ref, out_ref):
    rows = landed_ref.shape[1] // 2
    total = landed_ref[:NEARS].astype(F32)
    for y in range(1, YH):
        total = total + landed_ref[y * NEARS : (y + 1) * NEARS].astype(F32)
    total = total * (1.0 / REPLICAS)
    out_ref[:, :rows] = total[:, :rows]
    left = total[:, rows:, :RANK] + total[:, rows:, RANK:]
    half = rows // 2
    out_ref[:, rows:] = jnp.concatenate([left[:, :half], left[:, half:]], axis=2)


def terms_kernel(means_ref, out_ref, left_ref):
    near, rows = means_ref.shape[1], left_ref.shape[0] // NEARS
    core = lax.axis_index("core")

    def left_of(which):
        pieces = []
        for n in range(near):
            piece = means_ref[which, n, rows:]
            pieces += [piece[:, :RANK], piece[:, RANK:]]
        return jnp.concatenate(pieces, axis=0)

    def mean_of(which):
        return jnp.concatenate([means_ref[which, n, :rows] for n in range(near)], axis=0)

    mine, other = left_of(core), left_of(1 - core)
    left_ref[...] = mine
    left = jnp.concatenate([mine, other], axis=0)
    mean = jnp.concatenate([mean_of(core), mean_of(1 - core)], axis=0)
    mean = jnp.where(core == 0, mean[:, :RANK], mean[:, RANK:])
    terms = lax.dot_general(
        left,
        jnp.concatenate([left, mean], axis=1),
        (((0,), (0,)), ((), ())),
        precision=EXACT,
        preferred_element_type=F32,
    )
    quarter = HALF // 2
    third, fourth = terms[HALF : HALF + quarter], terms[HALF + quarter :]
    middle = jnp.concatenate([third[:, HALF:RANK], fourth[:, HALF:RANK], third[:, RANK:]], axis=1)
    last = jnp.concatenate([fourth[: quarter // 2, RANK:], fourth[quarter // 2 :, RANK:]], axis=1)
    for z in range(Z):
        out_ref[z, :HALF] = terms[:HALF]
        out_ref[z, HALF : HALF + quarter] = middle
        out_ref[z, HALF + quarter :] = last


def factor_kernel(landed_ref, left_ref, q_ref, ortho_ref, held):
    sums = landed_ref[0]
    for z in range(1, Z):
        sums = sums + landed_ref[z]
    upper = sums[:HALF]
    middle = sums[HALF : HALF + HALF // 2]
    last = sums[HALF + HALF // 2 :]
    across = upper.T[HALF:RANK]
    rest = jnp.zeros((HALF // 2, RANK), F32)
    gram = jnp.concatenate(
        [
            upper,
            jnp.concatenate([across[: HALF // 2], middle[:, :HALF], rest], axis=1),
            jnp.concatenate([across[HALF // 2 :], middle[:, HALF:RANK], rest], axis=1),
        ],
        axis=0,
    )
    q_sum = jnp.concatenate(
        [upper[:, RANK:], middle[:, RANK:], last[:, :RANK], last[:, RANK:]], axis=0
    )
    lane = lax.broadcasted_iota(jnp.int32, (8, 2 * RANK), 1)
    sub = lax.broadcasted_iota(jnp.int32, (8, 2 * RANK), 0)
    blocks = []
    for b in range(RANK // 8):
        unit = (lane == sub + RANK + 8 * b).astype(F32)
        blocks.append(jnp.where(lane < RANK, gram[8 * b : 8 * b + 8], unit))

    def lane_copy(value, column):
        return jnp.broadcast_to(value[:, column : column + 1], value.shape)

    def row_copy(slot, row):
        return jnp.broadcast_to(held[slot, row : row + 1, :], (8, 2 * RANK))

    inverse_rows = []
    for b in range(RANK // 8):
        here = blocks[b]
        columns = [lane_copy(here, 8 * b + j) for j in range(8)]
        later = [
            [lane_copy(blocks[t], 8 * b + j) for j in range(8)] for t in range(b + 1, RANK // 8)
        ]
        base = 9 * (b % 2)
        held[base + 8] = here
        for k in range(8):
            held[base + k] = columns[k]
        entry = [[row_copy(base + k, i) for k in range(i + 1)] for i in range(8)]
        row = [row_copy(base + 8, i) for i in range(8)]
        recip = [None] * 8
        factor = [[None] * 8 for _ in range(8)]
        for j in range(8):
            recip[j] = 1.0 / entry[j][j]
            for i in range(j + 1, 8):
                factor[i][j] = entry[i][j] * recip[j]
            for i in range(j + 1, 8):
                for k in range(j + 1, i + 1):
                    entry[i][k] = entry[i][k] - factor[i][j] * entry[k][j]
                row[i] = row[i] - factor[i][j] * row[j]
        done = row[0] * jnp.sqrt(recip[0])
        for i in range(1, 8):
            done = jnp.where(sub == i, row[i] * jnp.sqrt(recip[i]), done)
        inverse_rows.append(done)
        if b + 1 == RANK // 8:
            break
        solved = [row[i] * recip[i] for i in range(8)]
        for i in range(7, 0, -1):
            for j in range(i):
                solved[j] = solved[j] - factor[i][j] * solved[i]
        for t in range(b + 1, RANK // 8):
            update = later[t - b - 1][0] * solved[0]
            for j in range(1, 8):
                update = update + later[t - b - 1][j] * solved[j]
            blocks[t] = blocks[t] - update
    inverse = jnp.concatenate(inverse_rows, axis=0)[:, RANK:]

    q_mine = jnp.dot(inverse, q_sum, precision=EXACT, preferred_element_type=F32).astype(BF16)
    q_upper, q_lower = q_mine[:HALF], q_mine[HALF:]
    q_mine = jnp.where(
        lax.axis_index("core") == 0,
        jnp.concatenate([q_upper, q_lower], axis=1),
        jnp.concatenate([q_lower, q_upper], axis=1),
    )
    for peer in range(q_ref.shape[0]):
        q_ref[peer] = q_mine
    ortho_ref[...] = lax.dot_general(
        left_ref[...],
        inverse,
        (((1,), (1,)), ((), ())),
        precision=EXACT,
        preferred_element_type=F32,
    ).astype(BF16)


def rebuild_kernel(
    q_ref,
    ortho_ref,
    merged,
    error_hbm,
    own_hbm,
    q_next_hbm,
    q_all,
    error,
    own,
    q_next,
    out_sems,
    small_sems,
):
    cols = q_ref.shape[3]
    col_count = merged.shape[1]
    wide = col_count // SPANS
    outs = []
    for i in range(SPANS):
        span = pl.ds(i * wide, wide)
        outs.append(
            pltpu.make_async_copy(error.at[:, span], error_hbm.at[0, :, span], out_sems.at[i])
        )
    ortho = ortho_ref[...]
    lane = lax.broadcasted_iota(jnp.int32, (HALF, cols), 1)

    def upper_of(d):
        return jnp.where(lane < RANK, q_ref[0, d], q_ref[1, d])

    def lower_of(d):
        mixed = jnp.where(lane < RANK, q_ref[1, d], q_ref[0, d])
        return jnp.concatenate([mixed[:, RANK:], mixed[:, :RANK]], axis=1)

    mine = (lax.axis_index("yh") * YL + lax.axis_index("yl")) * X + lax.axis_index("x")
    right = jnp.concatenate([upper_of(mine), lower_of(mine)], axis=0)
    own[...] = jnp.dot(ortho, right, preferred_element_type=F32).astype(BF16)
    own_copy = pltpu.make_async_copy(own, own_hbm, small_sems.at[0])
    own_copy.start()
    count = q_next.shape[1] // cols
    first = (lax.axis_index("z") * CORES + lax.axis_index("core")) * count
    for i in range(count):
        q_next[:HALF, i * cols : (i + 1) * cols] = upper_of(first + i).astype(F32)
        q_next[HALF:, i * cols : (i + 1) * cols] = lower_of(first + i).astype(F32)
    q_next_copy = pltpu.make_async_copy(q_next, q_next_hbm, small_sems.at[1])
    q_next_copy.start()

    for i in range(SPANS):
        span = slice(i * wide, (i + 1) * wide)
        for d in range(i * wide // cols, (i + 1) * wide // cols):
            block = slice(d * cols, (d + 1) * cols)
            q_all[:HALF, block] = upper_of(d)
            q_all[HALF:, block] = lower_of(d)
        approx = jnp.dot(ortho, q_all[:, span], preferred_element_type=F32)
        error[:, span] = (merged[:, span].astype(F32) - approx).astype(BF16)
        outs[i].start()
    own_copy.wait()
    q_next_copy.wait()
    for i in range(SPANS):
        outs[i].wait()


def rebuild(q_all, ortho, merged, shard):
    rows, col_count = merged.shape
    cols = q_all.shape[3]
    return pl.pallas_call(
        rebuild_kernel,
        out_shape=(
            shape(BF16, 1, rows, col_count),
            shape(BF16, rows, cols),
            shape(F32, RANK, shard),
        ),
        in_specs=[VMEM, VMEM, VMEM],
        out_specs=[ANY, ANY, ANY],
        scratch_shapes=[
            pltpu.VMEM((RANK, col_count), BF16),
            pltpu.VMEM((rows, col_count), BF16),
            pltpu.VMEM((rows, cols), BF16),
            pltpu.VMEM((RANK, shard), F32),
            pltpu.SemaphoreType.DMA((SPANS,)),
            pltpu.SemaphoreType.DMA((2,)),
        ],
        compiler_params=pltpu.CompilerParams(vmem_limit_bytes=LIMIT),
    )(q_all, ortho, merged)


def on_device(grad, error, q_warm):
    rows, col_count = grad.shape[1:]
    cols = col_count // REPLICAS
    part = rows // NEARS
    merged = merge(grad, error)

    landed = lax.all_to_all(merged.reshape(NEARS, part, col_count), NEAR, 0, 0)
    warm = lax.all_gather(q_warm.astype(BF16), FSDP, axis=1, tiled=True)
    shares = call(left_kernel, shape(BF16, REPLICAS, 2 * part, cols), landed, warm)
    shares = lax.all_to_all(shares, DP, 0, 0)
    means = call(mean_kernel, shape(F32, NEARS, part + part // 2, cols), shares)
    terms, left = call(
        terms_kernel,
        (shape(F32, Z, RANK - 8, 2 * RANK), shape(F32, rows, RANK)),
        lax.all_gather(means, "core"),
    )
    terms = lax.all_to_all(terms, "z", 0, 0)
    q_copies, ortho = call(
        factor_kernel,
        (shape(BF16, REPLICAS, HALF, cols), shape(BF16, rows, RANK)),
        terms,
        left,
        scratch=[pltpu.VMEM((18, 8, 2 * RANK), F32)],
    )
    q_all = lax.all_gather(lax.all_to_all(q_copies, DP, 0, 0), "core")
    return rebuild(q_all, ortho, merged, q_warm.shape[1])


def solution(mesh):
    grid = Mesh(mesh.devices.reshape(YH, YL, X, Z, CORES), DP + FSDP)
    return jax.shard_map(
        on_device,
        mesh=grid,
        in_specs=(P(DP, FSDP, None), P(DP, FSDP, None), P(None, FSDP)),
        out_specs=(P(DP, FSDP, None), P(FSDP, DP), P(None, FSDP)),
        check_vma=False,
    )
```

```python
import jax
import jax.numpy as jnp
from jax import lax
from jax.experimental import pallas as pl
from jax.experimental.pallas import tpu as pltpu
from jax.sharding import Mesh, PartitionSpec as P

YH, YL, X, Z, CORES = 4, 2, 4, 8, 2
NEAR = ("yl", "x")
DP = ("yh", "yl", "x")
FSDP = ("z", "core")
NEARS = YL * X
CUTS = (3, 3, 1, 1)
SPANS = (1, 2, 2, 2, 1)


def pieces(sizes, whole):
    unit = whole // sum(sizes)
    return [(sum(sizes[:i]) * unit, sizes[i] * unit) for i in range(len(sizes))]


REPLICAS = YH * YL * X
RANK = 64
HALF = RANK // 2
EXACT = lax.Precision.HIGHEST
F32, BF16 = jnp.float32, jnp.bfloat16
VMEM = pl.BlockSpec(memory_space=pltpu.VMEM)
ANY = pl.BlockSpec(memory_space=pl.ANY)
LIMIT = 32 * 1024 * 1024


def call(kernel, out, *operands, scratch=()):
    many = isinstance(out, (list, tuple))
    return pl.pallas_call(
        kernel,
        out_shape=out,
        in_specs=[VMEM] * len(operands),
        out_specs=[VMEM] * len(out) if many else VMEM,
        scratch_shapes=list(scratch),
        compiler_params=pltpu.CompilerParams(vmem_limit_bytes=LIMIT),
    )(*operands)


def shape(dtype, *dims):
    return jax.ShapeDtypeStruct(dims, dtype)


def merge_kernel(grad_hbm, error_hbm, merged_hbm, grad, error, merged, in_sems, out_sems):
    cuts = pieces(CUTS, merged.shape[0])
    copies = []
    for i, (start, size) in enumerate(cuts):
        span = pl.ds(start, size)
        copies.append(
            (
                pltpu.make_async_copy(grad_hbm.at[0, span], grad.at[span], in_sems.at[0, i]),
                pltpu.make_async_copy(error_hbm.at[0, span], error.at[span], in_sems.at[1, i]),
                pltpu.make_async_copy(merged.at[span], merged_hbm.at[span], out_sems.at[i]),
            )
        )
        copies[i][0].start()
        copies[i][1].start()
    for i, (start, size) in enumerate(cuts):
        copies[i][0].wait()
        copies[i][1].wait()
        span = pl.ds(start, size)
        merged[span] = (grad[span].astype(F32) + error[span].astype(F32)).astype(BF16)
        copies[i][2].start()
    for copy in copies:
        copy[2].wait()


def merge(grad, error):
    _, rows, col_count = grad.shape
    return pl.pallas_call(
        merge_kernel,
        out_shape=shape(BF16, rows, col_count),
        in_specs=[ANY, ANY],
        out_specs=ANY,
        scratch_shapes=[pltpu.VMEM((rows, col_count), BF16)] * 3
        + [pltpu.SemaphoreType.DMA((2, len(CUTS))), pltpu.SemaphoreType.DMA((len(CUTS),))],
        compiler_params=pltpu.CompilerParams(vmem_limit_bytes=60 * 1024 * 1024),
    )(grad, error)


def fold(square):
    return jnp.concatenate([square[:HALF], square[HALF:]], axis=1)


def left_kernel(landed_ref, warm_ref, out_ref):
    near, rows, col_count = landed_ref.shape
    stacked = landed_ref[...].reshape(near * rows, col_count)
    every = lax.dot_general(
        stacked, warm_ref[...], (((1,), (1,)), ((), ())), preferred_element_type=F32
    )
    left = every[:rows]
    for n in range(1, near):
        left = left + every[n * rows : (n + 1) * rows]
    high = left.astype(BF16)
    left = jnp.concatenate([high, (left - high.astype(F32)).astype(BF16)], axis=1)
    cols = col_count // REPLICAS
    for d in range(REPLICAS):
        span = pl.ds(d * cols, cols)
        total = landed_ref[0, :, span].astype(F32)
        for n in range(1, near):
            total = total + landed_ref[n, :, span].astype(F32)
        out_ref[d, :rows] = total.astype(BF16)
        out_ref[d, rows:] = left


def mean_kernel(landed_ref, out_ref):
    rows = landed_ref.shape[1] // 2
    total = landed_ref[:NEARS].astype(F32)
    for y in range(1, YH):
        total = total + landed_ref[y * NEARS : (y + 1) * NEARS].astype(F32)
    total = total * (1.0 / REPLICAS)
    out_ref[:, :rows] = total[:, :rows]
    left = total[:, rows:, :RANK] + total[:, rows:, RANK:]
    half = rows // 2
    out_ref[:, rows:] = jnp.concatenate([left[:, :half], left[:, half:]], axis=2)


def terms_kernel(means_ref, out_ref, left_ref):
    near, rows = means_ref.shape[1], left_ref.shape[0] // NEARS
    core = lax.axis_index("core")

    def left_of(which):
        pieces = []
        for n in range(near):
            piece = means_ref[which, n, rows:]
            pieces += [piece[:, :RANK], piece[:, RANK:]]
        return jnp.concatenate(pieces, axis=0)

    def mean_of(which):
        return jnp.concatenate([means_ref[which, n, :rows] for n in range(near)], axis=0)

    mine, other = left_of(core), left_of(1 - core)
    left_ref[...] = mine
    left = jnp.concatenate([mine, other], axis=0)
    mean = jnp.concatenate([mean_of(core), mean_of(1 - core)], axis=0)
    mean = jnp.where(core == 0, mean[:, :RANK], mean[:, RANK:])
    terms = lax.dot_general(
        left,
        jnp.concatenate([left, mean], axis=1),
        (((0,), (0,)), ((), ())),
        precision=EXACT,
        preferred_element_type=F32,
    )
    quarter = HALF // 2
    third, fourth = terms[HALF : HALF + quarter], terms[HALF + quarter :]
    middle = jnp.concatenate([third[:, HALF:RANK], fourth[:, HALF:RANK], third[:, RANK:]], axis=1)
    last = jnp.concatenate([fourth[: quarter // 2, RANK:], fourth[quarter // 2 :, RANK:]], axis=1)
    for z in range(Z):
        out_ref[z, :HALF] = terms[:HALF]
        out_ref[z, HALF : HALF + quarter] = middle
        out_ref[z, HALF + quarter :] = last


def factor_kernel(landed_ref, left_ref, q_ref, ortho_ref, held):
    sums = landed_ref[0]
    for z in range(1, Z):
        sums = sums + landed_ref[z]
    upper = sums[:HALF]
    middle = sums[HALF : HALF + HALF // 2]
    last = sums[HALF + HALF // 2 :]
    across = upper.T[HALF:RANK]
    rest = jnp.zeros((HALF // 2, RANK), F32)
    gram = jnp.concatenate(
        [
            upper,
            jnp.concatenate([across[: HALF // 2], middle[:, :HALF], rest], axis=1),
            jnp.concatenate([across[HALF // 2 :], middle[:, HALF:RANK], rest], axis=1),
        ],
        axis=0,
    )
    q_sum = jnp.concatenate(
        [upper[:, RANK:], middle[:, RANK:], last[:, :RANK], last[:, RANK:]], axis=0
    )
    lane = lax.broadcasted_iota(jnp.int32, (8, 2 * RANK), 1)
    sub = lax.broadcasted_iota(jnp.int32, (8, 2 * RANK), 0)
    blocks = []
    for b in range(RANK // 8):
        unit = (lane == sub + RANK + 8 * b).astype(F32)
        blocks.append(jnp.where(lane < RANK, gram[8 * b : 8 * b + 8], unit))

    def lane_copy(value, column):
        return jnp.broadcast_to(value[:, column : column + 1], value.shape)

    def row_copy(slot, row):
        return jnp.broadcast_to(held[slot, row : row + 1, :], (8, 2 * RANK))

    inverse_rows = []
    for b in range(RANK // 8):
        here = blocks[b]
        columns = [lane_copy(here, 8 * b + j) for j in range(8)]
        later = [
            [lane_copy(blocks[t], 8 * b + j) for j in range(8)] for t in range(b + 1, RANK // 8)
        ]
        base = 9 * (b % 2)
        held[base + 8] = here
        for k in range(8):
            held[base + k] = columns[k]
        entry = [[row_copy(base + k, i) for k in range(i + 1)] for i in range(8)]
        row = [row_copy(base + 8, i) for i in range(8)]
        recip = [None] * 8
        factor = [[None] * 8 for _ in range(8)]
        for j in range(8):
            recip[j] = 1.0 / entry[j][j]
            for i in range(j + 1, 8):
                factor[i][j] = entry[i][j] * recip[j]
            for i in range(j + 1, 8):
                for k in range(j + 1, i + 1):
                    entry[i][k] = entry[i][k] - factor[i][j] * entry[k][j]
                row[i] = row[i] - factor[i][j] * row[j]
        done = row[0] * jnp.sqrt(recip[0])
        for i in range(1, 8):
            done = jnp.where(sub == i, row[i] * jnp.sqrt(recip[i]), done)
        inverse_rows.append(done)
        if b + 1 == RANK // 8:
            break
        solved = [row[i] * recip[i] for i in range(8)]
        for i in range(7, 0, -1):
            for j in range(i):
                solved[j] = solved[j] - factor[i][j] * solved[i]
        for t in range(b + 1, RANK // 8):
            update = later[t - b - 1][0] * solved[0]
            for j in range(1, 8):
                update = update + later[t - b - 1][j] * solved[j]
            blocks[t] = blocks[t] - update
    inverse = jnp.concatenate(inverse_rows, axis=0)[:, RANK:]

    q_mine = jnp.dot(inverse, q_sum, precision=EXACT, preferred_element_type=F32).astype(BF16)
    q_upper, q_lower = q_mine[:HALF], q_mine[HALF:]
    q_mine = jnp.where(
        lax.axis_index("core") == 0,
        jnp.concatenate([q_upper, q_lower], axis=1),
        jnp.concatenate([q_lower, q_upper], axis=1),
    )
    for peer in range(q_ref.shape[0]):
        q_ref[peer] = q_mine
    ortho_ref[...] = lax.dot_general(
        left_ref[...],
        inverse,
        (((1,), (1,)), ((), ())),
        precision=EXACT,
        preferred_element_type=F32,
    ).astype(BF16)


def rebuild_kernel(
    q_ref,
    ortho_ref,
    merged,
    error_hbm,
    own_hbm,
    q_next_hbm,
    q_all,
    error,
    own,
    q_next,
    out_sems,
    small_sems,
):
    cols = q_ref.shape[3]
    col_count = merged.shape[1]
    spans = pieces(SPANS, col_count)
    outs = []
    for i, (start, wide) in enumerate(spans):
        span = pl.ds(start, wide)
        outs.append(
            pltpu.make_async_copy(error.at[:, span], error_hbm.at[0, :, span], out_sems.at[i])
        )
    ortho = ortho_ref[...]
    lane = lax.broadcasted_iota(jnp.int32, (HALF, cols), 1)

    def upper_of(d):
        return jnp.where(lane < RANK, q_ref[0, d], q_ref[1, d])

    def lower_of(d):
        mixed = jnp.where(lane < RANK, q_ref[1, d], q_ref[0, d])
        return jnp.concatenate([mixed[:, RANK:], mixed[:, :RANK]], axis=1)

    mine = (lax.axis_index("yh") * YL + lax.axis_index("yl")) * X + lax.axis_index("x")
    right = jnp.concatenate([upper_of(mine), lower_of(mine)], axis=0)
    own[...] = jnp.dot(ortho, right, preferred_element_type=F32).astype(BF16)
    own_copy = pltpu.make_async_copy(own, own_hbm, small_sems.at[0])
    own_copy.start()
    count = q_next.shape[1] // cols
    first = (lax.axis_index("z") * CORES + lax.axis_index("core")) * count
    for i in range(count):
        q_next[:HALF, i * cols : (i + 1) * cols] = upper_of(first + i).astype(F32)
        q_next[HALF:, i * cols : (i + 1) * cols] = lower_of(first + i).astype(F32)
    q_next_copy = pltpu.make_async_copy(q_next, q_next_hbm, small_sems.at[1])
    q_next_copy.start()

    for i, (start, wide) in enumerate(spans):
        span = slice(start, start + wide)
        for d in range(start // cols, (start + wide) // cols):
            block = slice(d * cols, (d + 1) * cols)
            q_all[:HALF, block] = upper_of(d)
            q_all[HALF:, block] = lower_of(d)
        approx = jnp.dot(ortho, q_all[:, span], preferred_element_type=F32)
        error[:, span] = (merged[:, span].astype(F32) - approx).astype(BF16)
        outs[i].start()
    own_copy.wait()
    q_next_copy.wait()
    for out in outs:
        out.wait()


def rebuild(q_all, ortho, merged, shard):
    rows, col_count = merged.shape
    cols = q_all.shape[3]
    return pl.pallas_call(
        rebuild_kernel,
        out_shape=(
            shape(BF16, 1, rows, col_count),
            shape(BF16, rows, cols),
            shape(F32, RANK, shard),
        ),
        in_specs=[VMEM, VMEM, VMEM],
        out_specs=[ANY, ANY, ANY],
        scratch_shapes=[
            pltpu.VMEM((RANK, col_count), BF16),
            pltpu.VMEM((rows, col_count), BF16),
            pltpu.VMEM((rows, cols), BF16),
            pltpu.VMEM((RANK, shard), F32),
            pltpu.SemaphoreType.DMA((len(SPANS),)),
            pltpu.SemaphoreType.DMA((2,)),
        ],
        compiler_params=pltpu.CompilerParams(vmem_limit_bytes=LIMIT),
    )(q_all, ortho, merged)


def on_device(grad, error, q_warm):
    rows, col_count = grad.shape[1:]
    cols = col_count // REPLICAS
    part = rows // NEARS
    merged = merge(grad, error)

    landed = lax.all_to_all(merged.reshape(NEARS, part, col_count), NEAR, 0, 0)
    warm = lax.all_gather(q_warm.astype(BF16), FSDP, axis=1, tiled=True)
    shares = call(left_kernel, shape(BF16, REPLICAS, 2 * part, cols), landed, warm)
    shares = lax.all_to_all(shares, DP, 0, 0)
    means = call(mean_kernel, shape(F32, NEARS, part + part // 2, cols), shares)
    terms, left = call(
        terms_kernel,
        (shape(F32, Z, RANK - 8, 2 * RANK), shape(F32, rows, RANK)),
        lax.all_gather(means, "core"),
    )
    terms = lax.all_to_all(terms, "z", 0, 0)
    q_copies, ortho = call(
        factor_kernel,
        (shape(BF16, REPLICAS, HALF, cols), shape(BF16, rows, RANK)),
        terms,
        left,
        scratch=[pltpu.VMEM((18, 8, 2 * RANK), F32)],
    )
    q_all = lax.all_gather(lax.all_to_all(q_copies, DP, 0, 0), "core")
    return rebuild(q_all, ortho, merged, q_warm.shape[1])


def solution(mesh):
    grid = Mesh(mesh.devices.reshape(YH, YL, X, Z, CORES), DP + FSDP)
    return jax.shard_map(
        on_device,
        mesh=grid,
        in_specs=(P(DP, FSDP, None), P(DP, FSDP, None), P(None, FSDP)),
        out_specs=(P(DP, FSDP, None), P(FSDP, DP), P(None, FSDP)),
        check_vma=False,
    )
```

```python
import jax
import jax.numpy as jnp
from jax import lax
from jax.experimental import pallas as pl
from jax.experimental.pallas import tpu as pltpu
from jax.sharding import Mesh, PartitionSpec as P

YH, YL, X, Z, CORES = 4, 2, 4, 8, 2
NEAR = ("yl", "x")
DP = ("yh", "yl", "x")
FSDP = ("z", "core")
NEARS = YL * X
CUTS = (3, 3, 1, 1)
SPANS = (1, 2, 2, 2, 1)


def pieces(sizes, whole):
    unit = whole // sum(sizes)
    return [(sum(sizes[:i]) * unit, sizes[i] * unit) for i in range(len(sizes))]


REPLICAS = YH * YL * X
RANK = 64
HALF = RANK // 2
EXACT = lax.Precision.HIGHEST
F32, BF16 = jnp.float32, jnp.bfloat16
VMEM = pl.BlockSpec(memory_space=pltpu.VMEM)
ANY = pl.BlockSpec(memory_space=pl.ANY)
LIMIT = 32 * 1024 * 1024


def call(kernel, out, *operands, scratch=()):
    many = isinstance(out, (list, tuple))
    return pl.pallas_call(
        kernel,
        out_shape=out,
        in_specs=[VMEM] * len(operands),
        out_specs=[VMEM] * len(out) if many else VMEM,
        scratch_shapes=list(scratch),
        compiler_params=pltpu.CompilerParams(vmem_limit_bytes=LIMIT),
    )(*operands)


def shape(dtype, *dims):
    return jax.ShapeDtypeStruct(dims, dtype)


def merge_kernel(
    grad_hbm, error_hbm, q_hbm, merged_hbm, warm_ref, grad, error, merged, q, in_sems, out_sems, q_sem
):
    q_copy = pltpu.make_async_copy(q_hbm, q, q_sem)
    cuts = pieces(CUTS, merged.shape[0])
    copies = []
    for i, (start, size) in enumerate(cuts):
        span = pl.ds(start, size)
        copies.append(
            (
                pltpu.make_async_copy(grad_hbm.at[0, span], grad.at[span], in_sems.at[0, i]),
                pltpu.make_async_copy(error_hbm.at[0, span], error.at[span], in_sems.at[1, i]),
                pltpu.make_async_copy(merged.at[span], merged_hbm.at[span], out_sems.at[i]),
            )
        )
        copies[i][0].start()
        copies[i][1].start()
    q_copy.start()
    for i, (start, size) in enumerate(cuts):
        copies[i][0].wait()
        copies[i][1].wait()
        span = pl.ds(start, size)
        merged[span] = (grad[span].astype(F32) + error[span].astype(F32)).astype(BF16)
        copies[i][2].start()
    q_copy.wait()
    warm_ref[...] = q[...].astype(BF16)
    for copy in copies:
        copy[2].wait()


def merge(grad, error, q_warm):
    _, rows, col_count = grad.shape
    return pl.pallas_call(
        merge_kernel,
        out_shape=(shape(BF16, rows, col_count), shape(BF16, *q_warm.shape)),
        in_specs=[ANY, ANY, ANY],
        out_specs=[ANY, VMEM],
        scratch_shapes=[pltpu.VMEM((rows, col_count), BF16)] * 3
        + [
            pltpu.VMEM(q_warm.shape, F32),
            pltpu.SemaphoreType.DMA((2, len(CUTS))),
            pltpu.SemaphoreType.DMA((len(CUTS),)),
            pltpu.SemaphoreType.DMA,
        ],
        compiler_params=pltpu.CompilerParams(vmem_limit_bytes=60 * 1024 * 1024),
    )(grad, error, q_warm)


def fold(square):
    return jnp.concatenate([square[:HALF], square[HALF:]], axis=1)


def left_kernel(landed_ref, warm_ref, out_ref):
    near, rows, col_count = landed_ref.shape
    stacked = landed_ref[...].reshape(near * rows, col_count)
    every = lax.dot_general(
        stacked, warm_ref[...], (((1,), (1,)), ((), ())), preferred_element_type=F32
    )
    left = every[:rows]
    for n in range(1, near):
        left = left + every[n * rows : (n + 1) * rows]
    high = left.astype(BF16)
    left = jnp.concatenate([high, (left - high.astype(F32)).astype(BF16)], axis=1)
    cols = col_count // REPLICAS
    for d in range(REPLICAS):
        span = pl.ds(d * cols, cols)
        total = landed_ref[0, :, span].astype(F32)
        for n in range(1, near):
            total = total + landed_ref[n, :, span].astype(F32)
        out_ref[d, :rows] = total.astype(BF16)
        out_ref[d, rows:] = left


def mean_kernel(landed_ref, out_ref):
    rows = landed_ref.shape[1] // 2
    total = landed_ref[:NEARS].astype(F32)
    for y in range(1, YH):
        total = total + landed_ref[y * NEARS : (y + 1) * NEARS].astype(F32)
    total = total * (1.0 / REPLICAS)
    out_ref[:, :rows] = total[:, :rows]
    left = total[:, rows:, :RANK] + total[:, rows:, RANK:]
    half = rows // 2
    out_ref[:, rows:] = jnp.concatenate([left[:, :half], left[:, half:]], axis=2)


def terms_kernel(means_ref, out_ref, left_ref):
    near, rows = means_ref.shape[1], left_ref.shape[0] // NEARS
    core = lax.axis_index("core")

    def left_of(which):
        pieces = []
        for n in range(near):
            piece = means_ref[which, n, rows:]
            pieces += [piece[:, :RANK], piece[:, RANK:]]
        return jnp.concatenate(pieces, axis=0)

    def mean_of(which):
        return jnp.concatenate([means_ref[which, n, :rows] for n in range(near)], axis=0)

    mine, other = left_of(core), left_of(1 - core)
    left_ref[...] = mine
    left = jnp.concatenate([mine, other], axis=0)
    mean = jnp.concatenate([mean_of(core), mean_of(1 - core)], axis=0)
    mean = jnp.where(core == 0, mean[:, :RANK], mean[:, RANK:])
    terms = lax.dot_general(
        left,
        jnp.concatenate([left, mean], axis=1),
        (((0,), (0,)), ((), ())),
        precision=EXACT,
        preferred_element_type=F32,
    )
    quarter = HALF // 2
    third, fourth = terms[HALF : HALF + quarter], terms[HALF + quarter :]
    middle = jnp.concatenate([third[:, HALF:RANK], fourth[:, HALF:RANK], third[:, RANK:]], axis=1)
    last = jnp.concatenate([fourth[: quarter // 2, RANK:], fourth[quarter // 2 :, RANK:]], axis=1)
    for z in range(Z):
        out_ref[z, :HALF] = terms[:HALF]
        out_ref[z, HALF : HALF + quarter] = middle
        out_ref[z, HALF + quarter :] = last


def factor_kernel(landed_ref, left_ref, q_ref, ortho_ref, held):
    sums = landed_ref[0]
    for z in range(1, Z):
        sums = sums + landed_ref[z]
    upper = sums[:HALF]
    middle = sums[HALF : HALF + HALF // 2]
    last = sums[HALF + HALF // 2 :]
    across = upper.T[HALF:RANK]
    rest = jnp.zeros((HALF // 2, RANK), F32)
    gram = jnp.concatenate(
        [
            upper,
            jnp.concatenate([across[: HALF // 2], middle[:, :HALF], rest], axis=1),
            jnp.concatenate([across[HALF // 2 :], middle[:, HALF:RANK], rest], axis=1),
        ],
        axis=0,
    )
    q_sum = jnp.concatenate(
        [upper[:, RANK:], middle[:, RANK:], last[:, :RANK], last[:, RANK:]], axis=0
    )
    lane = lax.broadcasted_iota(jnp.int32, (8, 2 * RANK), 1)
    sub = lax.broadcasted_iota(jnp.int32, (8, 2 * RANK), 0)
    blocks = []
    for b in range(RANK // 8):
        unit = (lane == sub + RANK + 8 * b).astype(F32)
        blocks.append(jnp.where(lane < RANK, gram[8 * b : 8 * b + 8], unit))

    def lane_copy(value, column):
        return jnp.broadcast_to(value[:, column : column + 1], value.shape)

    def row_copy(slot, row):
        return jnp.broadcast_to(held[slot, row : row + 1, :], (8, 2 * RANK))

    inverse_rows = []
    for b in range(RANK // 8):
        here = blocks[b]
        columns = [lane_copy(here, 8 * b + j) for j in range(8)]
        later = [
            [lane_copy(blocks[t], 8 * b + j) for j in range(8)] for t in range(b + 1, RANK // 8)
        ]
        base = 9 * (b % 2)
        held[base + 8] = here
        for k in range(8):
            held[base + k] = columns[k]
        entry = [[row_copy(base + k, i) for k in range(i + 1)] for i in range(8)]
        row = [row_copy(base + 8, i) for i in range(8)]
        recip = [None] * 8
        factor = [[None] * 8 for _ in range(8)]
        for j in range(8):
            recip[j] = 1.0 / entry[j][j]
            for i in range(j + 1, 8):
                factor[i][j] = entry[i][j] * recip[j]
            for i in range(j + 1, 8):
                for k in range(j + 1, i + 1):
                    entry[i][k] = entry[i][k] - factor[i][j] * entry[k][j]
                row[i] = row[i] - factor[i][j] * row[j]
        done = row[0] * jnp.sqrt(recip[0])
        for i in range(1, 8):
            done = jnp.where(sub == i, row[i] * jnp.sqrt(recip[i]), done)
        inverse_rows.append(done)
        if b + 1 == RANK // 8:
            break
        solved = [row[i] * recip[i] for i in range(8)]
        for i in range(7, 0, -1):
            for j in range(i):
                solved[j] = solved[j] - factor[i][j] * solved[i]
        for t in range(b + 1, RANK // 8):
            update = later[t - b - 1][0] * solved[0]
            for j in range(1, 8):
                update = update + later[t - b - 1][j] * solved[j]
            blocks[t] = blocks[t] - update
    inverse = jnp.concatenate(inverse_rows, axis=0)[:, RANK:]

    q_mine = jnp.dot(inverse, q_sum, precision=EXACT, preferred_element_type=F32).astype(BF16)
    q_upper, q_lower = q_mine[:HALF], q_mine[HALF:]
    q_mine = jnp.where(
        lax.axis_index("core") == 0,
        jnp.concatenate([q_upper, q_lower], axis=1),
        jnp.concatenate([q_lower, q_upper], axis=1),
    )
    for peer in range(q_ref.shape[0]):
        q_ref[peer] = q_mine
    ortho_ref[...] = lax.dot_general(
        left_ref[...],
        inverse,
        (((1,), (1,)), ((), ())),
        precision=EXACT,
        preferred_element_type=F32,
    ).astype(BF16)


def rebuild_kernel(
    q_ref,
    ortho_ref,
    merged,
    error_hbm,
    own_hbm,
    q_next_hbm,
    q_all,
    error,
    own,
    q_next,
    out_sems,
    small_sems,
):
    cols = q_ref.shape[3]
    col_count = merged.shape[1]
    spans = pieces(SPANS, col_count)
    outs = []
    for i, (start, wide) in enumerate(spans):
        span = pl.ds(start, wide)
        outs.append(
            pltpu.make_async_copy(error.at[:, span], error_hbm.at[0, :, span], out_sems.at[i])
        )
    ortho = ortho_ref[...]
    lane = lax.broadcasted_iota(jnp.int32, (HALF, cols), 1)

    def upper_of(d):
        return jnp.where(lane < RANK, q_ref[0, d], q_ref[1, d])

    def lower_of(d):
        mixed = jnp.where(lane < RANK, q_ref[1, d], q_ref[0, d])
        return jnp.concatenate([mixed[:, RANK:], mixed[:, :RANK]], axis=1)

    mine = (lax.axis_index("yh") * YL + lax.axis_index("yl")) * X + lax.axis_index("x")
    right = jnp.concatenate([upper_of(mine), lower_of(mine)], axis=0)
    own[...] = jnp.dot(ortho, right, preferred_element_type=F32).astype(BF16)
    own_copy = pltpu.make_async_copy(own, own_hbm, small_sems.at[0])
    own_copy.start()
    count = q_next.shape[1] // cols
    first = (lax.axis_index("z") * CORES + lax.axis_index("core")) * count
    for i in range(count):
        q_next[:HALF, i * cols : (i + 1) * cols] = upper_of(first + i).astype(F32)
        q_next[HALF:, i * cols : (i + 1) * cols] = lower_of(first + i).astype(F32)
    q_next_copy = pltpu.make_async_copy(q_next, q_next_hbm, small_sems.at[1])
    q_next_copy.start()

    for i, (start, wide) in enumerate(spans):
        span = slice(start, start + wide)
        for d in range(start // cols, (start + wide) // cols):
            block = slice(d * cols, (d + 1) * cols)
            q_all[:HALF, block] = upper_of(d)
            q_all[HALF:, block] = lower_of(d)
        approx = jnp.dot(ortho, q_all[:, span], preferred_element_type=F32)
        error[:, span] = (merged[:, span].astype(F32) - approx).astype(BF16)
        outs[i].start()
    own_copy.wait()
    q_next_copy.wait()
    for out in outs:
        out.wait()


def rebuild(q_all, ortho, merged, shard):
    rows, col_count = merged.shape
    cols = q_all.shape[3]
    return pl.pallas_call(
        rebuild_kernel,
        out_shape=(
            shape(BF16, 1, rows, col_count),
            shape(BF16, rows, cols),
            shape(F32, RANK, shard),
        ),
        in_specs=[VMEM, VMEM, VMEM],
        out_specs=[ANY, ANY, ANY],
        scratch_shapes=[
            pltpu.VMEM((RANK, col_count), BF16),
            pltpu.VMEM((rows, col_count), BF16),
            pltpu.VMEM((rows, cols), BF16),
            pltpu.VMEM((RANK, shard), F32),
            pltpu.SemaphoreType.DMA((len(SPANS),)),
            pltpu.SemaphoreType.DMA((2,)),
        ],
        compiler_params=pltpu.CompilerParams(vmem_limit_bytes=LIMIT),
    )(q_all, ortho, merged)


def on_device(grad, error, q_warm):
    rows, col_count = grad.shape[1:]
    cols = col_count // REPLICAS
    part = rows // NEARS
    merged, warm = merge(grad, error, q_warm)

    landed = lax.all_to_all(merged.reshape(NEARS, part, col_count), NEAR, 0, 0)
    warm = lax.all_gather(warm, FSDP, axis=1, tiled=True)
    shares = call(left_kernel, shape(BF16, REPLICAS, 2 * part, cols), landed, warm)
    shares = lax.all_to_all(shares, DP, 0, 0)
    means = call(mean_kernel, shape(F32, NEARS, part + part // 2, cols), shares)
    terms, left = call(
        terms_kernel,
        (shape(F32, Z, RANK - 8, 2 * RANK), shape(F32, rows, RANK)),
        lax.all_gather(means, "core"),
    )
    terms = lax.all_to_all(terms, "z", 0, 0)
    q_copies, ortho = call(
        factor_kernel,
        (shape(BF16, REPLICAS, HALF, cols), shape(BF16, rows, RANK)),
        terms,
        left,
        scratch=[pltpu.VMEM((18, 8, 2 * RANK), F32)],
    )
    q_all = lax.all_gather(lax.all_to_all(q_copies, DP, 0, 0), "core")
    return rebuild(q_all, ortho, merged, q_warm.shape[1])


def solution(mesh):
    grid = Mesh(mesh.devices.reshape(YH, YL, X, Z, CORES), DP + FSDP)
    return jax.shard_map(
        on_device,
        mesh=grid,
        in_specs=(P(DP, FSDP, None), P(DP, FSDP, None), P(None, FSDP)),
        out_specs=(P(DP, FSDP, None), P(FSDP, DP), P(None, FSDP)),
        check_vma=False,
    )
```
